32 devices in a mesh: ctx: 16 (over z, y, x), head: 2 (over core).
Axes of the slice: x: 2, y: 2, z: 4, core: 2. Of those that a mesh axis runs over, the one named last changes fastest.
Arguments:
- document_query: bfloat16 [4096, 8192], P('ctx', 'head'), may hold values from -6 to 6
- document_keys: bfloat16 [4096, 1024], P('ctx', 'head'), may hold values from -4 to 4
- document_values: bfloat16 [4096, 1024], P('ctx', 'head'), may hold values from -6 to 6
- question_query: bfloat16 [128, 8192], P(None, 'head'), may hold values from -10 to 10
- prompt_keys: bfloat16 [128, 1024], P(None, 'head'), may hold values from -6 to 6
- prompt_values: bfloat16 [128, 1024], P(None, 'head'), may hold values from -6 to 6
- out_weight: bfloat16 [8192, 8192], P('head', 'ctx'), may hold values from -0.0625 to 0.0625
Outputs:
- doc_attention: bfloat16 [4096, 8192], P('ctx', 'head')
- question_out: bfloat16 [128, 8192], P('head', 'ctx')
The draws below stay inside these ranges and needn't reach their ends.
All inputs are finite; a program needn't handle non-finite values.
Results may differ from the reference program's by a relative error of at most 0.014.
Values may be sent and summed in bfloat16 or wider, within the bound.
No kernel may reach another device: no remote copies, remote signals or barrier semaphores. Data moves between devices by JAX's collectives and lax.ppermute only.
A program may use at most 64 MiB of HBM per device.

```python
import jax
import jax.numpy as jnp
from jax import lax

D = 8192
QUERY_HEADS = 64
KEY_VALUE_HEADS = 8
HEAD_SIZE = 128
BLOCK_TOKENS = 256
QUESTION_TOKENS = 128
ANCHOR_TOKENS = 256
DOCUMENT_TOKENS = 4096
N_CTX = 16


def drawn_queries(key, salt_value, row_total, spread):
    own_key = jax.random.fold_in(key, salt_value)
    column_count_total = QUERY_HEADS * HEAD_SIZE
    return jax.random.truncated_normal(own_key, -4.0, 4.0, (row_total, column_count_total), jnp.float32) * spread


def draw_document_query(key, part):
    return drawn_queries(key, 11, DOCUMENT_TOKENS, 1.5).astype(jnp.bfloat16)


def draw_question_query(key, part):
    values = drawn_queries(key, 17, QUESTION_TOKENS, 2.5)
    return values.astype(jnp.bfloat16)


def draw_document_keys(key, part):
    own_key = jax.random.fold_in(key, 23)
    column_count_total = KEY_VALUE_HEADS * HEAD_SIZE
    return jax.random.truncated_normal(own_key, -4.0, 4.0, (DOCUMENT_TOKENS, column_count_total), jnp.float32).astype(jnp.bfloat16)


def levels(rng, dims, cuts, smallest, top_value):
    def one(axis_at, parts):
        heights = jax.random.uniform(jax.random.fold_in(jax.random.fold_in(rng, 6), axis_at), (parts,), jnp.float32, smallest / len(cuts), top_value / len(cuts))
        return jnp.repeat(jnp.exp(heights), dims[axis_at] // parts).reshape((-1,) + (1,) * (len(dims) - axis_at - 1))

    gain = one(*cuts[0])
    for cut in cuts[1:]:
        gain = gain * one(*cut)
    return gain


def centred(stream_key, extent, deviation, reach, pieces=(), kind=jnp.bfloat16):
    level = levels(stream_key, extent, pieces, -0.22, 0.18) if pieces else 1.0
    drawn = jax.random.normal(stream_key, extent, jnp.float32) * deviation * level
    return jnp.minimum(jnp.maximum(drawn, -reach), reach).astype(kind)


def setup_inputs(seed: int = 0) -> dict:
    keys = jax.random.split(jax.random.key(seed), 8)
    return {
        "document_query": draw_document_query(jax.random.fold_in(keys[7], 71), 0),
        "document_keys": draw_document_keys(jax.random.fold_in(keys[7], 71), 0),
        "document_values": centred(keys[2], (DOCUMENT_TOKENS, KEY_VALUE_HEADS * HEAD_SIZE), 1.0, 6.0, ((0, 16), (1, 2))),
        "question_query": draw_question_query(jax.random.fold_in(keys[7], 71), 0),
        "prompt_keys": centred(keys[4], (QUESTION_TOKENS, KEY_VALUE_HEADS * HEAD_SIZE), 1.5, 6.0, ((1, 2),)),
        "prompt_values": centred(keys[5], (QUESTION_TOKENS, KEY_VALUE_HEADS * HEAD_SIZE), 1.0, 6.0, ((1, 2),)),
        "out_weight": centred(keys[6], (QUERY_HEADS * HEAD_SIZE, D), (QUERY_HEADS * HEAD_SIZE) ** -0.5, 0.0625, ((0, 2), (1, 16))),
    }


def rounded(values):
    return lax.optimization_barrier(values.astype(jnp.bfloat16)).astype(jnp.float32)


def reference(document_query, document_keys, document_values, question_query, prompt_keys, prompt_values, out_weight):
    factor = HEAD_SIZE ** -0.5
    query_group_width = QUERY_HEADS // KEY_VALUE_HEADS
    leading_keys = document_keys[:ANCHOR_TOKENS].astype(jnp.float32).reshape(ANCHOR_TOKENS, KEY_VALUE_HEADS, HEAD_SIZE)
    leading_values = document_values[:ANCHOR_TOKENS].astype(jnp.float32).reshape(ANCHOR_TOKENS, KEY_VALUE_HEADS, HEAD_SIZE)
    block_ids = jnp.arange(BLOCK_TOKENS, dtype=jnp.int32)
    causal = block_ids[:, None] >= block_ids[None, :]

    def one_block(block_index):
        starting_row = (block_index * BLOCK_TOKENS).astype(jnp.int32)
        query_rows = lax.dynamic_slice_in_dim(document_query, starting_row, BLOCK_TOKENS, 0).astype(jnp.float32).reshape(BLOCK_TOKENS, KEY_VALUE_HEADS, query_group_width, HEAD_SIZE)
        block_own_keys = lax.dynamic_slice_in_dim(document_keys, starting_row, BLOCK_TOKENS, 0).astype(jnp.float32).reshape(BLOCK_TOKENS, KEY_VALUE_HEADS, HEAD_SIZE)
        block_own_values = lax.dynamic_slice_in_dim(document_values, starting_row, BLOCK_TOKENS, 0).astype(jnp.float32).reshape(BLOCK_TOKENS, KEY_VALUE_HEADS, HEAD_SIZE)
        anchor_scores = jnp.einsum("qhgd,khd->hgqk", query_rows, leading_keys) * factor
        anchor_scores = jnp.where(block_index > 0, anchor_scores, -jnp.inf)
        own_scores = jnp.einsum("qhgd,khd->hgqk", query_rows, block_own_keys) * factor
        own_scores = jnp.where(causal, own_scores, -jnp.inf)
        row_top = jnp.maximum(anchor_scores.max(axis=3, keepdims=True), own_scores.max(axis=3, keepdims=True))
        anchor_exp = jnp.exp(anchor_scores - row_top)
        own_exp = jnp.exp(own_scores - row_top)
        denominator = anchor_exp.sum(axis=3) + own_exp.sum(axis=3)
        mixture = jnp.einsum("hgqk,khd->hgqd", rounded(anchor_exp), leading_values)
        mixture = mixture + jnp.einsum("hgqk,khd->hgqd", rounded(own_exp), block_own_values)
        result = mixture / denominator[..., None]
        return jnp.transpose(result, (2, 0, 1, 3)).reshape(BLOCK_TOKENS, QUERY_HEADS * HEAD_SIZE).astype(jnp.bfloat16)

    doc_attention = lax.map(one_block, jnp.arange(N_CTX, dtype=jnp.int32)).reshape(N_CTX * BLOCK_TOKENS, QUERY_HEADS * HEAD_SIZE)

    question_ids = jnp.arange(QUESTION_TOKENS, dtype=jnp.int32)
    self_visible = question_ids[:, None] >= question_ids[None, :]

    def single_head(kv_head):
        column = (kv_head * HEAD_SIZE).astype(jnp.int32)
        query_column = (kv_head * query_group_width * HEAD_SIZE).astype(jnp.int32)
        query_rows = lax.dynamic_slice_in_dim(question_query, query_column, query_group_width * HEAD_SIZE, 1).astype(jnp.float32).reshape(QUESTION_TOKENS, query_group_width, HEAD_SIZE)
        block_keys = lax.dynamic_slice_in_dim(document_keys, column, HEAD_SIZE, 1).astype(jnp.float32).reshape(N_CTX, BLOCK_TOKENS, HEAD_SIZE)
        block_values = lax.dynamic_slice_in_dim(document_values, column, HEAD_SIZE, 1).astype(jnp.float32).reshape(N_CTX, BLOCK_TOKENS, HEAD_SIZE)
        scores = jnp.einsum("qgd,ckd->cgqk", query_rows, block_keys) * factor
        block_max = scores.max(axis=3)
        exp_scores = jnp.exp(scores - block_max[..., None])
        block_total = exp_scores.sum(axis=3)
        block_sums = jnp.einsum("cgqk,ckd->cgqd", rounded(exp_scores), block_values)
        self_keys = lax.dynamic_slice_in_dim(prompt_keys, column, HEAD_SIZE, 1).astype(jnp.float32)
        self_values = lax.dynamic_slice_in_dim(prompt_values, column, HEAD_SIZE, 1).astype(jnp.float32)
        self_scores = jnp.einsum("qgd,kd->gqk", query_rows, self_keys) * factor
        self_scores = jnp.where(self_visible, self_scores, -jnp.inf)
        self_max = self_scores.max(axis=2)
        self_exp = jnp.exp(self_scores - self_max[..., None])
        self_total = self_exp.sum(axis=2)
        self_sums = jnp.einsum("gqk,kd->gqd", rounded(self_exp), self_values)
        row_top = jnp.maximum(block_max.max(axis=0), self_max)
        block_weights = jnp.exp(block_max - row_top)
        self_weights = jnp.exp(self_max - row_top)
        denominator = (block_total * block_weights).sum(axis=0) + self_total * self_weights
        numerator = (block_sums * block_weights[..., None]).sum(axis=0) + self_sums * self_weights[..., None]
        return (numerator / denominator[..., None]).astype(jnp.bfloat16)

    head_outputs = lax.map(single_head, jnp.arange(KEY_VALUE_HEADS, dtype=jnp.int32))
    question_attention = jnp.transpose(head_outputs, (2, 0, 1, 3)).reshape(QUESTION_TOKENS, QUERY_HEADS * HEAD_SIZE)
    question_out = jnp.dot(question_attention, out_weight, preferred_element_type=jnp.float32).astype(jnp.bfloat16)
    return doc_attention, question_out
```

```python
import functools
import math

import jax
import jax.numpy as jnp
from jax import lax
from jax.experimental import pallas as pl
from jax.experimental.pallas import tpu as pltpu
from jax.sharding import PartitionSpec as P

QUERY_HEADS = 64
KEY_VALUE_HEADS = 8
HEAD_SIZE = 128
GROUP_WIDTH = QUERY_HEADS // KEY_VALUE_HEADS
FACTOR = HEAD_SIZE**-0.5
LOG2E = math.log2(math.e)
NEG_INF = float("-inf")
STAT_ROWS = 16
VMEM = pl.BlockSpec(memory_space=pltpu.VMEM)
SMEM = pl.BlockSpec(memory_space=pltpu.SMEM)
PARAMS = pltpu.CompilerParams(vmem_limit_bytes=32 * 1024 * 1024)


def dot_nt(left, right):
    return lax.dot_general(
        left, right, (((1,), (1,)), ((), ())), preferred_element_type=jnp.float32
    )


def dot_nn(left, right):
    return jnp.dot(left, right, preferred_element_type=jnp.float32)


def with_ones(values):
    return jnp.concatenate([values, jnp.ones_like(values)], axis=1)


def transposed_with_ones(values):
    flipped = values.astype(jnp.float32).T.astype(jnp.bfloat16)
    return jnp.concatenate([flipped, jnp.ones((STAT_ROWS, values.shape[0]), jnp.bfloat16)], axis=0)


def columns(index, width):
    return pl.ds(pl.multiple_of(index * width, width), width)


def cut_pieces(place, keys, values, group):
    token_count = keys.shape[0]

    def kernel(place_ref, keys_ref, values_ref, *pieces):
        for step, piece in enumerate(pieces):
            cut = columns(place_ref[0] ^ step, HEAD_SIZE)
            piece[0] = keys_ref[:, cut]
            piece[1] = values_ref[:, cut]

    shape = jax.ShapeDtypeStruct((2, token_count, HEAD_SIZE), keys.dtype)
    return pl.pallas_call(
        kernel,
        out_shape=[shape] * group,
        in_specs=[SMEM, VMEM, VMEM],
        out_specs=[VMEM] * group,
        compiler_params=PARAMS,
        name="cut_pieces",
    )(place, keys, values)


def stat_rows(top, total):
    high = total.astype(jnp.bfloat16).astype(jnp.float32)
    at = lax.broadcasted_iota(jnp.int32, (STAT_ROWS, top.shape[1]), 0)
    low = jnp.where(at == 2, total - high, 0.0)
    return jnp.where(at == 0, top, jnp.where(at == 1, high, low)).astype(jnp.bfloat16)


def question_parts(place, question_query, pieces, ring):
    group = len(pieces)
    row_count = question_query.shape[0]
    head_total = question_query.shape[1] // HEAD_SIZE
    unit_heads = head_total // (group * ring)
    unit_columns = unit_heads * HEAD_SIZE
    unit_rows = unit_heads * row_count

    def kernel(place_ref, query_ref, *refs):
        piece_refs, outs = refs[:group], refs[group:]
        keys = jnp.concatenate([piece[0] for piece in piece_refs], axis=0)
        values = transposed_with_ones(jnp.concatenate([piece[1] for piece in piece_refs], axis=0))
        for step, out in enumerate(outs):
            heads = query_ref[:, columns(place_ref[1] ^ step, unit_columns)]
            queries = jnp.concatenate(
                [heads[:, i * HEAD_SIZE : (i + 1) * HEAD_SIZE] for i in range(unit_heads)], axis=0
            )
            scores = dot_nt(keys, queries)
            top = scores.max(axis=0, keepdims=True) * FACTOR
            top = top.astype(jnp.bfloat16).astype(jnp.float32)
            weights = jnp.exp2(scores * (FACTOR * LOG2E) - top * LOG2E)
            sums = dot_nn(values, weights.astype(jnp.bfloat16))
            out[:HEAD_SIZE] = sums[:HEAD_SIZE].astype(jnp.bfloat16)
            out[HEAD_SIZE:] = stat_rows(top, sums[HEAD_SIZE : HEAD_SIZE + 1])

    def whole(shape):
        return pl.BlockSpec(shape, lambda i, place_ref: (0,) * len(shape))

    out_shape = (HEAD_SIZE + STAT_ROWS, unit_rows)
    return pl.pallas_call(
        kernel,
        out_shape=[jax.ShapeDtypeStruct(out_shape, jnp.bfloat16)] * ring,
        grid_spec=pltpu.PrefetchScalarGridSpec(
            num_scalar_prefetch=1,
            grid=(1,),
            in_specs=[
                pl.BlockSpec(
                    (row_count, ring * unit_columns), lambda i, place_ref: (0, place_ref[0])
                )
            ]
            + [whole(pieces[0].shape)] * group,
            out_specs=[whole(out_shape)] * ring,
        ),
        compiler_params=PARAMS,
        name="question_parts",
    )(place, question_query, *pieces)


def prompt_part(place, question_query, prompt_keys, prompt_values, group, ring):
    row_count = question_query.shape[0]
    key_count = prompt_keys.shape[0]
    head_total = question_query.shape[1] // HEAD_SIZE
    unit_heads = head_total // (group * ring)
    unit_columns = unit_heads * HEAD_SIZE
    unit_rows = unit_heads * row_count

    def kernel(place_ref, query_ref, keys_ref, values_ref, out):
        queries = jnp.concatenate(
            [query_ref[:, i * HEAD_SIZE : (i + 1) * HEAD_SIZE] for i in range(unit_heads)], axis=0
        )
        scores = dot_nt(keys_ref[...], queries)
        key_ids = lax.broadcasted_iota(jnp.int32, (key_count, unit_rows), 0)
        row_ids = lax.broadcasted_iota(jnp.int32, (key_count, unit_rows), 1) % row_count
        scores = jnp.where(key_ids <= row_ids, scores * FACTOR, NEG_INF)
        top = scores.max(axis=0, keepdims=True)
        weights = jnp.exp(scores - top)
        total = weights.sum(axis=0, keepdims=True)
        values = values_ref[...].astype(jnp.float32).T.astype(jnp.bfloat16)
        out[:HEAD_SIZE] = dot_nn(values, weights.astype(jnp.bfloat16))
        at = lax.broadcasted_iota(jnp.int32, (8, unit_rows), 0)
        out[HEAD_SIZE:] = jnp.where(at == 0, top, total)

    out_shape = (HEAD_SIZE + 8, unit_rows)
    return pl.pallas_call(
        kernel,
        out_shape=jax.ShapeDtypeStruct(out_shape, jnp.float32),
        grid_spec=pltpu.PrefetchScalarGridSpec(
            num_scalar_prefetch=1,
            grid=(1,),
            in_specs=[
                pl.BlockSpec(
                    (row_count, unit_columns),
                    lambda i, place_ref: (0, place_ref[0] * ring + place_ref[1]),
                ),
                pl.BlockSpec((key_count, HEAD_SIZE), lambda i, place_ref: (0, place_ref[0])),
                pl.BlockSpec((key_count, HEAD_SIZE), lambda i, place_ref: (0, place_ref[0])),
            ],
            out_specs=pl.BlockSpec(out_shape, lambda i, place_ref: (0, 0)),
        ),
        compiler_params=PARAMS,
        name="prompt_part",
    )(place, question_query, prompt_keys, prompt_values)


def merge_parts(parts, prompt, row_count):
    unit_rows = prompt.shape[1]
    unit_heads = unit_rows // row_count

    def kernel(prompt_ref, *refs):
        part_refs, out = refs[:-1], refs[-1]
        tops, totals, sums = [], [], []
        stats = prompt_ref[HEAD_SIZE:]
        tops.append(stats[0:1])
        totals.append(stats[1:2])
        sums.append(prompt_ref[:HEAD_SIZE])
        for part in part_refs:
            stats = part[HEAD_SIZE:].astype(jnp.float32)
            tops.append(stats[0:1])
            totals.append(stats[1:2] + stats[2:3])
            sums.append(part[:HEAD_SIZE].astype(jnp.float32))
        row_top = functools.reduce(jnp.maximum, tops)
        scales = [jnp.exp(top - row_top) for top in tops]
        total = sum(scale * value for scale, value in zip(scales, totals))
        merged = sum(scale * value for scale, value in zip(scales, sums)) / total
        for i in range(unit_heads):
            out[:, i * HEAD_SIZE : (i + 1) * HEAD_SIZE] = merged[
                :, i * row_count : (i + 1) * row_count
            ].T.astype(jnp.bfloat16)

    return pl.pallas_call(
        kernel,
        out_shape=jax.ShapeDtypeStruct((row_count, unit_heads * HEAD_SIZE), jnp.bfloat16),
        in_specs=[VMEM] * (1 + len(parts)),
        out_specs=VMEM,
        compiler_params=PARAMS,
        name="merge_parts",
    )(prompt, *parts)


def project(blocks, chunks, weight, partial=None, splits=None, own_split=None):
    row_count, depth = chunks[0].shape[0], chunks[0].shape[1]
    counts = []
    for chunk in chunks:
        counts.append(chunk.shape[0] // row_count if chunk.ndim == 2 else chunk.shape[0])
    row_count = min(chunk.shape[0] for chunk in chunks) if partial is None else partial.shape[0]
    counts = [chunk.shape[0] // row_count for chunk in chunks]
    chunk_total = sum(counts)
    width = weight.shape[1]
    first = partial is None

    def kernel(blocks_ref, weight_ref, *refs):
        chunk_refs = refs[: len(chunks)]
        refs = refs[len(chunks) :]
        if first:
            out, held, sems = refs
        else:
            split_ref, partial_ref = refs[:2]
            outs, (total_ref, held, sems) = refs[2:-3], refs[-3:]
        copies = []
        for at in range(chunk_total):
            start = pl.multiple_of(blocks_ref[at] * depth, depth)
            copies.append(
                pltpu.make_async_copy(
                    weight_ref.at[pl.ds(start, depth)], held.at[at], sems.at[at]
                )
            )
            copies[-1].start()
        total = None if first else partial_ref[...]
        at = 0
        for chunk, count in zip(chunk_refs, counts):
            for i in range(count):
                copies[at].wait()
                term = dot_nn(chunk[i * row_count : (i + 1) * row_count], held[at])
                total = term if total is None else total + term
                at += 1
        if first:
            out[...] = total
        else:
            total_ref[...] = total
            span = row_count // splits
            for step, out in enumerate(outs):
                place = split_ref[0] ^ step
                out[...] = total_ref[pl.ds(pl.multiple_of(place * span, span), span)].astype(
                    out.dtype
                )

    scratch = [
        pltpu.VMEM((chunk_total, depth, width), weight.dtype),
        pltpu.SemaphoreType.DMA((chunk_total,)),
    ]
    in_specs = [SMEM, pl.BlockSpec(memory_space=pl.ANY)] + [VMEM] * len(chunks)
    operands = [blocks, weight, *chunks]
    if first:
        out_shape = jax.ShapeDtypeStruct((row_count, width), jnp.float32)
        out_specs = VMEM
    else:
        in_specs += [SMEM, VMEM]
        operands += [own_split, partial]
        scratch = [pltpu.VMEM((row_count, width), jnp.float32)] + scratch
        out_shape = [
            jax.ShapeDtypeStruct(
                (row_count // splits, width), jnp.float32 if step == 0 else jnp.bfloat16
            )
            for step in range(splits)
        ]
        out_specs = [VMEM] * splits
    return pl.pallas_call(
        kernel,
        out_shape=out_shape,
        in_specs=in_specs,
        out_specs=out_specs,
        scratch_shapes=scratch,
        compiler_params=PARAMS,
        name="project",
    )(*operands)


def document_heads(place, query, keys, values, anchor, written, step_heads=4):
    token_count = query.shape[0]
    half = token_count // 2
    step_columns = step_heads * HEAD_SIZE
    steps = GROUP_WIDTH // step_heads
    scale = FACTOR * LOG2E

    def kernel(place_ref, query_ref, keys_ref, values_ref, anchor_ref, *refs):
        out = refs[-1]
        after_anchor = place_ref[1] > 0
        anchor_keys, anchor_values = anchor_ref[0], with_ones(anchor_ref[1])
        own_keys, own_values = keys_ref[...], with_ones(values_ref[...])
        row_ids = lax.broadcasted_iota(jnp.int32, (half, half), 0)
        key_ids = lax.broadcasted_iota(jnp.int32, (half, half), 1)
        visible = row_ids >= key_ids
        for head in range(step_heads):
            cut = slice(head * HEAD_SIZE, (head + 1) * HEAD_SIZE)
            for part in range(2):
                rows = slice(part * half, (part + 1) * half)
                queries = query_ref[rows, cut]
                anchor_scores = dot_nt(queries, anchor_keys)
                own_scores = dot_nt(queries, own_keys[: (part + 1) * half])
                last = jnp.where(visible, own_scores[:, part * half :], NEG_INF)
                if part:
                    own_scores = jnp.concatenate([own_scores[:, :half], last], axis=1)
                else:
                    own_scores = last
                own_top = own_scores.max(axis=1, keepdims=True)
                anchor_top = anchor_scores.max(axis=1, keepdims=True)
                top = jnp.where(after_anchor, jnp.maximum(own_top, anchor_top), own_top) * scale
                anchor_shift = jnp.where(after_anchor, top, 1e30)
                anchor_exp = jnp.exp2(anchor_scores * scale - anchor_shift).astype(jnp.bfloat16)
                own_exp = jnp.exp2(own_scores * scale - top).astype(jnp.bfloat16)
                mixture = dot_nn(anchor_exp, anchor_values)
                mixture = mixture + dot_nn(own_exp, own_values[: (part + 1) * half])
                out[rows, cut] = (mixture[:, :HEAD_SIZE] / mixture[:, HEAD_SIZE:]).astype(out.dtype)

    in_specs = [
        pl.BlockSpec((token_count, step_columns), lambda i, place_ref: (0, place_ref[0] * steps + i)),
        pl.BlockSpec((token_count, HEAD_SIZE), lambda i, place_ref: (0, place_ref[0])),
        pl.BlockSpec((token_count, HEAD_SIZE), lambda i, place_ref: (0, place_ref[0])),
        pl.BlockSpec(anchor.shape, lambda i, place_ref: (0, 0, 0)),
    ]
    operands = [place, query, keys, values, anchor]
    aliases = {}
    if written is not None:
        in_specs.append(pl.BlockSpec(memory_space=pl.ANY))
        operands.append(written)
        aliases = {len(operands) - 1: 0}
    return pl.pallas_call(
        kernel,
        out_shape=jax.ShapeDtypeStruct(query.shape, query.dtype),
        grid_spec=pltpu.PrefetchScalarGridSpec(
            num_scalar_prefetch=1,
            grid=(steps,),
            in_specs=in_specs,
            out_specs=pl.BlockSpec(
                (token_count, step_columns), lambda i, place_ref: (0, place_ref[0] * steps + i)
            ),
        ),
        input_output_aliases=aliases,
        compiler_params=PARAMS,
        name="document_heads",
    )(*operands)


def joined(*scalars):
    return jnp.stack([jnp.asarray(scalar, jnp.int32) for scalar in scalars])


def swapped(values, axis, size, step):
    return lax.ppermute(values, axis, [(place, place ^ step) for place in range(size)])


def question_by_reduction(query, keys, values, prompt_keys, prompt_values, weight):
    row_count = query.shape[0]
    kv_total = keys.shape[1] // HEAD_SIZE
    queries = query.reshape(row_count, kv_total, GROUP_WIDTH, HEAD_SIZE)

    def part(key_block, value_block, visible):
        key_block = key_block.reshape(-1, kv_total, HEAD_SIZE)
        value_block = value_block.reshape(-1, kv_total, HEAD_SIZE)
        scores = FACTOR * jnp.einsum(
            "qhgd,khd->hgqk", queries, key_block, preferred_element_type=jnp.float32
        )
        if visible is not None:
            scores = jnp.where(visible, scores, NEG_INF)
        top = scores.max(axis=3, keepdims=True)
        weights = jnp.exp(scores - top)
        sums = jnp.einsum(
            "hgqk,khd->hgqd",
            weights.astype(jnp.bfloat16),
            value_block,
            preferred_element_type=jnp.float32,
        )
        return top, weights.sum(axis=3, keepdims=True), sums

    ids = jnp.arange(row_count, dtype=jnp.int32)
    block_top, block_total, block_sums = part(keys, values, None)
    self_top, self_total, self_sums = part(prompt_keys, prompt_values, ids[:, None] >= ids[None, :])
    row_top = jnp.maximum(lax.pmax(block_top, "ctx"), self_top)
    scale = jnp.exp(block_top - row_top)
    total, sums = lax.psum((block_total * scale, block_sums * scale), "ctx")
    self_scale = jnp.exp(self_top - row_top)
    attention = (sums + self_sums * self_scale) / (total + self_total * self_scale)
    attention = attention.astype(jnp.bfloat16).transpose(2, 0, 1, 3).reshape(row_count, -1)
    return lax.psum_scatter(
        dot_nn(attention, weight).astype(jnp.bfloat16), "head", scatter_dimension=0, tiled=True
    )


def local(
    ctx_size,
    head_size,
    document_query,
    document_keys,
    document_values,
    question_query,
    prompt_keys,
    prompt_values,
    out_weight,
):
    group = document_keys.shape[1] // HEAD_SIZE
    ring = ctx_size // group
    row_count = question_query.shape[0]
    head_total = question_query.shape[1] // HEAD_SIZE
    position = lax.axis_index("ctx")
    member, turn = position % group, position // group
    place = joined(member, turn)

    pieces = cut_pieces(place, document_keys, document_values, group)
    pieces = [pieces[0]] + [
        swapped(pieces[step], "ctx", ctx_size, step) for step in range(1, group)
    ]

    anchor = lax.select_n(member, *pieces) if group > 1 else pieces[0]
    reach = ring // 2
    while reach:
        pairs = [
            (turn_at * group + at, (turn_at + reach) * group + at)
            for turn_at in range(0, ring, 2 * reach)
            for at in range(group)
        ]
        arrived = lax.ppermute(anchor, "ctx", pairs)
        anchor = jnp.where(turn % (2 * reach) == reach, arrived, anchor)
        reach //= 2
    anchors = [anchor] + [swapped(anchor, "ctx", ctx_size, step) for step in range(1, group)]

    doc_attention = None
    for step in range(group):
        doc_attention = document_heads(
            joined(member ^ step, position),
            document_query,
            document_keys,
            document_values,
            anchors[step],
            doc_attention,
        )

    if head_total % ctx_size:
        return doc_attention, question_by_reduction(
            question_query, document_keys, document_values, prompt_keys, prompt_values, out_weight
        )

    parts = question_parts(place, question_query, pieces, ring)
    prompt = prompt_part(place, question_query, prompt_keys, prompt_values, group, ring)
    parts = [parts[0]] + [
        swapped(parts[step], "ctx", ctx_size, step * group) for step in range(1, ring)
    ]
    attention = merge_parts(parts, prompt, row_count)

    def unit(group_step, ring_step):
        return (member ^ group_step) * ring + (turn ^ ring_step)

    around = [swapped(attention, "ctx", ctx_size, step * group) for step in range(1, ring)]
    beside = [swapped(attention, "ctx", ctx_size, step) for step in range(1, group)]
    first = project(
        joined(
            *[unit(0, step) for step in range(ring)], *[unit(step, 0) for step in range(1, group)]
        ),
        [attention, *around, *beside],
        out_weight,
    )
    passed = jnp.concatenate(around, axis=0)
    far = [swapped(passed, "ctx", ctx_size, step) for step in range(1, group)]
    shares = project(
        joined(
            *[unit(step, ring_step) for step in range(1, group) for ring_step in range(1, ring)]
        ),
        far,
        out_weight,
        partial=first,
        splits=head_size,
        own_split=joined(lax.axis_index("head")),
    )
    question_out = shares[0]
    for step in range(1, head_size):
        question_out = question_out + swapped(shares[step], "head", head_size, step).astype(
            jnp.float32
        )
    return doc_attention, question_out.astype(jnp.bfloat16)


def solution(mesh):
    placed = (
        P("ctx", "head"),
        P("ctx", "head"),
        P("ctx", "head"),
        P(None, "head"),
        P(None, "head"),
        P(None, "head"),
        P("head", "ctx"),
    )
    return jax.shard_map(
        functools.partial(local, mesh.shape["ctx"], mesh.shape["head"]),
        mesh=mesh,
        in_specs=placed,
        out_specs=(P("ctx", "head"), P("head", "ctx")),
        check_vma=False,
    )
```

```python
import functools
import math

import jax
import jax.numpy as jnp
from jax import lax
from jax.experimental import pallas as pl
from jax.experimental.pallas import tpu as pltpu
from jax.sharding import PartitionSpec as P

QUERY_HEADS = 64
KEY_VALUE_HEADS = 8
HEAD_SIZE = 128
GROUP_WIDTH = QUERY_HEADS // KEY_VALUE_HEADS
FACTOR = HEAD_SIZE**-0.5
LOG2E = math.log2(math.e)
NEG_INF = float("-inf")
STAT_ROWS = 16
VMEM = pl.BlockSpec(memory_space=pltpu.VMEM)
ANY = pl.BlockSpec(memory_space=pl.ANY)
SMEM = pl.BlockSpec(memory_space=pltpu.SMEM)
PARAMS = pltpu.CompilerParams(vmem_limit_bytes=32 * 1024 * 1024)


def dot_nt(left, right):
    return lax.dot_general(
        left, right, (((1,), (1,)), ((), ())), preferred_element_type=jnp.float32
    )


def dot_nn(left, right):
    return jnp.dot(left, right, preferred_element_type=jnp.float32)


def with_ones(values):
    return jnp.concatenate([values, jnp.ones_like(values)], axis=1)


def columns(index, width):
    return pl.ds(pl.multiple_of(index * width, width), width)


def in_hbm(values):
    return pltpu.with_memory_space_constraint(values, pltpu.MemorySpace.HBM)


def cut_pieces(place, keys, values, group, question=()):
    token_count = keys.shape[0]

    def kernel(place_ref, keys_ref, values_ref, *refs):
        question_refs, refs = refs[: len(question)], refs[len(question) :]
        pieces, cuts, sems = refs[:group], refs[group:-1], refs[-1]
        pairs = []
        for step, piece in enumerate(pieces):
            cut = columns(place_ref[0] ^ step, HEAD_SIZE)
            for half, source in enumerate((keys_ref, values_ref)):
                pairs.append((source.at[:, cut], piece.at[pl.ds(half * token_count, token_count)]))
        for source, target in zip(question_refs, cuts):
            pairs.append((source.at[:, columns(place_ref[0], target.shape[1])], target))
        copies = [
            pltpu.make_async_copy(source, target, sems.at[i])
            for i, (source, target) in enumerate(pairs)
        ]
        for copy in copies:
            copy.start()
        for copy in copies:
            copy.wait()

    shapes = [jax.ShapeDtypeStruct((2 * token_count, HEAD_SIZE), keys.dtype)] * group + [
        jax.ShapeDtypeStruct((array.shape[0], array.shape[1] // group), array.dtype)
        for array in question
    ]
    return pl.pallas_call(
        kernel,
        out_shape=shapes,
        in_specs=[SMEM] + [ANY] * (2 + len(question)),
        out_specs=[ANY] * len(shapes),
        scratch_shapes=[pltpu.SemaphoreType.DMA((len(shapes) + group,))],
        compiler_params=PARAMS,
        name="cut_pieces",
    )(place, in_hbm(keys), in_hbm(values), *map(in_hbm, question))


def question_parts(place, query, own_keys, own_values, pieces, ring):
    group = len(pieces)
    token_count = pieces[0].shape[0] // 2
    row_count, key_count = query.shape[0], own_keys.shape[0]
    unit_heads = query.shape[1] // (HEAD_SIZE * ring)
    unit_columns = unit_heads * HEAD_SIZE
    unit_rows = unit_heads * row_count
    out_shape = (unit_rows + STAT_ROWS, HEAD_SIZE)

    def kernel(place_ref, query_ref, own_keys_ref, own_values_ref, *refs):
        piece_refs, outs = refs[:group], refs[group:]
        all_keys = jnp.concatenate([piece[:token_count] for piece in piece_refs], axis=0)
        all_values = with_ones(jnp.concatenate([piece[token_count:] for piece in piece_refs], axis=0))
        own_keys, own_values = own_keys_ref[...], with_ones(own_values_ref[...])
        lanes = lax.broadcasted_iota(jnp.int32, (row_count, HEAD_SIZE), 1)
        stat_ids = lax.broadcasted_iota(jnp.int32, (STAT_ROWS, row_count), 0)
        visible = lax.broadcasted_iota(jnp.int32, (row_count, key_count), 0) >= (
            lax.broadcasted_iota(jnp.int32, (row_count, key_count), 1)
        )
        visible = jnp.concatenate([visible] * unit_heads, axis=0)
        for step, out in enumerate(outs):
            heads = query_ref[:, columns(place_ref[1] ^ step, unit_columns)]
            queries = jnp.concatenate(
                [heads[:, i * HEAD_SIZE : (i + 1) * HEAD_SIZE] for i in range(unit_heads)], axis=0
            )
            scores, values = dot_nt(queries, all_keys), all_values
            if step == 0:
                own_scores = jnp.where(visible, dot_nt(queries, own_keys), NEG_INF)
                scores = jnp.concatenate([scores, own_scores], axis=1)
                values = jnp.concatenate([values, own_values], axis=0)
            top = scores.max(axis=1, keepdims=True) * FACTOR
            top = top.astype(jnp.bfloat16).astype(jnp.float32)
            weights = jnp.exp2(scores * (FACTOR * LOG2E) - top * LOG2E)
            sums = dot_nn(weights.astype(jnp.bfloat16), values)
            out[:unit_rows] = sums[:, :HEAD_SIZE].astype(jnp.bfloat16)
            totals = sums[:, HEAD_SIZE:]
            stats = jnp.zeros((STAT_ROWS, row_count), jnp.float32)
            for i in range(unit_heads):
                rows = slice(i * row_count, (i + 1) * row_count)
                flipped = jnp.where(lanes < HEAD_SIZE // 2, top[rows], totals[rows]).T
                total = flipped[HEAD_SIZE // 2 : HEAD_SIZE // 2 + 1]
                high = total.astype(jnp.bfloat16).astype(jnp.float32)
                for j, value in enumerate((flipped[:1], high, total - high)):
                    stats = jnp.where(stat_ids == 3 * i + j, value, stats)
            out[unit_rows:] = stats.astype(jnp.bfloat16)

    return pl.pallas_call(
        kernel,
        out_shape=[jax.ShapeDtypeStruct(out_shape, jnp.bfloat16)] * ring,
        in_specs=[SMEM] + [VMEM] * (3 + group),
        out_specs=[VMEM] * ring,
        compiler_params=PARAMS,
        name="question_parts",
    )(place, query, own_keys, own_values, *pieces)


def merge_parts(parts, row_count):
    unit_rows = parts[0].shape[0] - STAT_ROWS
    unit_heads = unit_rows // row_count

    def kernel(*refs):
        part_refs, out = refs[:-1], refs[-1]
        stats = [part[unit_rows:].astype(jnp.float32).T for part in part_refs]
        for i in range(unit_heads):
            rows = slice(i * row_count, (i + 1) * row_count)
            tops = [stat[:, 3 * i : 3 * i + 1] for stat in stats]
            totals = [stat[:, 3 * i + 1 : 3 * i + 2] + stat[:, 3 * i + 2 : 3 * i + 3] for stat in stats]
            row_top = functools.reduce(jnp.maximum, tops)
            scales = [jnp.exp(top - row_top) for top in tops]
            total = sum(scale * value for scale, value in zip(scales, totals))
            merged = sum(
                scale * part[rows].astype(jnp.float32) for scale, part in zip(scales, part_refs)
            )
            out[rows] = (merged / total).astype(jnp.bfloat16)

    return pl.pallas_call(
        kernel,
        out_shape=jax.ShapeDtypeStruct((unit_rows, HEAD_SIZE), jnp.bfloat16),
        in_specs=[VMEM] * len(parts),
        out_specs=VMEM,
        compiler_params=PARAMS,
        name="merge_parts",
    )(*parts)


def project(blocks, chunks, weight, row_count, unit_heads, splits, own_split):
    depth, width = unit_heads * HEAD_SIZE, weight.shape[1]
    arrays, spots = [], []
    for array, start in chunks:
        if not any(array is other for other in arrays):
            arrays.append(array)
        spots.append((next(i for i, other in enumerate(arrays) if other is array), start))

    def kernel(blocks_ref, split_ref, weight_ref, *refs):
        array_refs, outs, total_ref = refs[: len(arrays)], refs[len(arrays) : -1], refs[-1]
        total = None
        for at, (which, start) in enumerate(spots):
            rows = jnp.concatenate(
                [
                    array_refs[which][start + i * row_count : start + (i + 1) * row_count]
                    for i in range(unit_heads)
                ],
                axis=1,
            )
            block = weight_ref[pl.ds(pl.multiple_of(blocks_ref[at] * depth, depth), depth)]
            term = dot_nn(rows, block)
            total = term if total is None else total + term
        total_ref[...] = total
        span = row_count // splits
        for step, out in enumerate(outs):
            start = pl.multiple_of((split_ref[0] ^ step) * span, span)
            out[...] = total_ref[pl.ds(start, span)].astype(out.dtype)

    return pl.pallas_call(
        kernel,
        out_shape=[
            jax.ShapeDtypeStruct(
                (row_count // splits, width), jnp.bfloat16 if step else jnp.float32
            )
            for step in range(splits)
        ],
        in_specs=[SMEM, SMEM, VMEM] + [VMEM] * len(arrays),
        out_specs=[VMEM] * splits,
        scratch_shapes=[pltpu.VMEM((row_count, width), jnp.float32)],
        compiler_params=PARAMS,
        name="project",
    )(blocks, own_split, weight, *arrays)


def document_heads(place, query, steps, own, anchors, written=None, weight=None):
    group = len(steps)
    token_count = query.shape[0]
    step_columns = GROUP_WIDTH * HEAD_SIZE
    scale = FACTOR * LOG2E
    extra = [array for array in (written, weight) if array is not None]

    def kernel(place_ref, query_ref, *refs):
        own_refs, anchor_refs = refs[:group], refs[group : 2 * group]
        extra_refs, refs = refs[2 * group :][: len(extra)], refs[2 * group + len(extra) :]
        out, refs = refs[0], refs[1:]
        bring = None
        if weight is not None:
            bring = pltpu.make_async_copy(extra_refs[-1], refs[0], refs[-1])
            refs = refs[1:]
        queries_ref, held, query_sems, sems = refs[:4]
        cuts = [columns(place_ref[0] ^ step, step_columns) for step in steps]
        fetches = [
            pltpu.make_async_copy(
                query_ref.at[:, cuts[step]], queries_ref.at[step], query_sems.at[step]
            )
            for step in range(group)
        ]
        for fetch in fetches:
            fetch.start()
        after_anchor = place_ref[1] > 0
        visible = lax.broadcasted_iota(jnp.int32, (token_count, token_count), 0) >= (
            lax.broadcasted_iota(jnp.int32, (token_count, token_count), 1)
        )
        copies = []
        for step in range(group):
            if step == 0:
                fetches[0].wait()
            if step == 1:
                for fetch in fetches[1:]:
                    fetch.wait()
                if bring is not None:
                    bring.start()
            pair = (anchor_refs[step], own_refs[step])
            all_keys = jnp.concatenate([ref[:token_count] for ref in pair], axis=0)
            all_values = with_ones(
                jnp.concatenate([ref[token_count : 2 * token_count] for ref in pair], axis=0)
            )
            for head in range(GROUP_WIDTH):
                spot = slice(head * HEAD_SIZE, (head + 1) * HEAD_SIZE)
                scores = dot_nt(queries_ref[step, :, spot], all_keys)
                anchor_scores = scores[:, :token_count]
                own_scores = jnp.where(visible, scores[:, token_count:], NEG_INF)
                own_top = own_scores.max(axis=1, keepdims=True)
                anchor_top = anchor_scores.max(axis=1, keepdims=True)
                top = jnp.where(after_anchor, jnp.maximum(own_top, anchor_top), own_top) * scale
                anchor_shift = jnp.where(after_anchor, top, 1e30)
                anchor_exp = jnp.exp2(anchor_scores * scale - anchor_shift).astype(jnp.bfloat16)
                own_exp = jnp.exp2(own_scores * scale - top).astype(jnp.bfloat16)
                mixture = dot_nn(jnp.concatenate([anchor_exp, own_exp], axis=1), all_values)
                held[step, :, spot] = (mixture[:, :HEAD_SIZE] / mixture[:, HEAD_SIZE:]).astype(
                    held.dtype
                )
            copies.append(
                pltpu.make_async_copy(held.at[step], out.at[:, cuts[step]], sems.at[step])
            )
            copies[-1].start()
        for copy in copies:
            copy.wait()
        if bring is not None:
            bring.wait()

    out_shape = [jax.ShapeDtypeStruct(query.shape, query.dtype)]
    if weight is not None:
        out_shape.append(jax.ShapeDtypeStruct(weight.shape, weight.dtype))
    return pl.pallas_call(
        kernel,
        out_shape=out_shape,
        in_specs=[SMEM, ANY] + [VMEM] * (2 * group) + [ANY] * len(extra),
        out_specs=[ANY] * len(out_shape),
        input_output_aliases={} if written is None else {2 + 2 * group: 0},
        scratch_shapes=[
            pltpu.VMEM((group, token_count, step_columns), query.dtype),
            pltpu.VMEM((group, token_count, step_columns), query.dtype),
            pltpu.SemaphoreType.DMA((group,)),
            pltpu.SemaphoreType.DMA((group,)),
            pltpu.SemaphoreType.DMA,
        ],
        compiler_params=PARAMS,
        name="document_heads",
    )(place, in_hbm(query), *own, *anchors, *map(in_hbm, extra))


def joined(*scalars):
    return jnp.stack([jnp.asarray(scalar, jnp.int32) for scalar in scalars])


def swapped(values, axis, size, step):
    return lax.ppermute(values, axis, [(place, place ^ step) for place in range(size)])


def question_by_reduction(query, keys, values, prompt_keys, prompt_values, weight):
    row_count = query.shape[0]
    kv_total = keys.shape[1] // HEAD_SIZE
    queries = query.reshape(row_count, kv_total, GROUP_WIDTH, HEAD_SIZE)

    def part(key_block, value_block, visible):
        key_block = key_block.reshape(-1, kv_total, HEAD_SIZE)
        value_block = value_block.reshape(-1, kv_total, HEAD_SIZE)
        scores = FACTOR * jnp.einsum(
            "qhgd,khd->hgqk", queries, key_block, preferred_element_type=jnp.float32
        )
        if visible is not None:
            scores = jnp.where(visible, scores, NEG_INF)
        top = scores.max(axis=3, keepdims=True)
        weights = jnp.exp(scores - top)
        sums = jnp.einsum(
            "hgqk,khd->hgqd",
            weights.astype(jnp.bfloat16),
            value_block,
            preferred_element_type=jnp.float32,
        )
        return top, weights.sum(axis=3, keepdims=True), sums

    ids = jnp.arange(row_count, dtype=jnp.int32)
    block_top, block_total, block_sums = part(keys, values, None)
    self_top, self_total, self_sums = part(prompt_keys, prompt_values, ids[:, None] >= ids[None, :])
    row_top = jnp.maximum(lax.pmax(block_top, "ctx"), self_top)
    scale = jnp.exp(block_top - row_top)
    total, sums = lax.psum((block_total * scale, block_sums * scale), "ctx")
    self_scale = jnp.exp(self_top - row_top)
    attention = (sums + self_sums * self_scale) / (total + self_total * self_scale)
    attention = attention.astype(jnp.bfloat16).transpose(2, 0, 1, 3).reshape(row_count, -1)
    return lax.psum_scatter(
        dot_nn(attention, weight).astype(jnp.bfloat16), "head", scatter_dimension=0, tiled=True
    )


def local(
    ctx_size,
    head_size,
    document_query,
    document_keys,
    document_values,
    question_query,
    prompt_keys,
    prompt_values,
    out_weight,
):
    group = document_keys.shape[1] // HEAD_SIZE
    ring = ctx_size // group
    row_count = question_query.shape[0]
    head_total = question_query.shape[1] // HEAD_SIZE
    position = lax.axis_index("ctx")
    member, turn = position % group, position // group
    place = joined(member, turn)

    def in_group(values, step):
        return swapped(values, "ctx", ctx_size, step)

    def in_ring(values, step):
        return swapped(values, "ctx", ctx_size, step * group)

    whole_units = head_total % ctx_size == 0
    question = (question_query, prompt_keys, prompt_values) if whole_units else ()
    cuts = cut_pieces(place, document_keys, document_values, group, question)
    pieces, question = cuts[:group], cuts[group:]
    own_pieces = pieces
    pieces = [pieces[0]] + [in_group(pieces[step], step) for step in range(1, group)]

    anchor = lax.select_n(member, *pieces) if group > 1 else pieces[0]

    def sent_on(anchor, reach):
        pairs = [
            (turn_at * group + at, (turn_at + reach) * group + at)
            for turn_at in range(0, ring, 2 * reach)
            for at in range(group)
        ]
        arrived = lax.ppermute(anchor, "ctx", pairs)
        return jnp.where(turn % (2 * reach) == reach, arrived, anchor)

    spot = joined(member, position)

    reach = ring // 2
    if not whole_units:
        while reach:
            anchor = sent_on(anchor, reach)
            reach //= 2
        anchors = [anchor] + [in_group(anchor, step) for step in range(1, group)]
        doc_attention = document_heads(
            spot, document_query, range(group), own_pieces, anchors
        )[0]
        return doc_attention, question_by_reduction(
            question_query, document_keys, document_values, prompt_keys, prompt_values, out_weight
        )

    unit_heads = head_total // ctx_size
    parts = question_parts(place, *question, pieces, ring)
    parts = [parts[0]] + [in_ring(parts[step], step) for step in range(1, ring)]
    while reach > 1:
        anchor = sent_on(anchor, reach)
        reach //= 2
    parts, anchor = lax.optimization_barrier((parts, anchor))
    attention = merge_parts(parts, row_count)
    if reach:
        anchor = sent_on(anchor, reach)
    shards = [attention] + [in_ring(attention, step) for step in range(1, ring)]

    chunks = [((0, step), shards[step], 0) for step in range(ring)]
    both = jnp.concatenate([anchor, attention], axis=0)
    passed = jnp.concatenate(shards[1:], axis=0)
    beside = [in_group(both, step) for step in range(1, group)]
    far = [in_group(passed, step) for step in range(1, group)]
    anchors = [anchor] + beside
    for member_step in range(1, group):
        chunks.append(((member_step, 0), beside[member_step - 1], anchor.shape[0]))
        for step in range(1, ring):
            chunks.append(
                ((member_step, step), far[member_step - 1], (step - 1) * attention.shape[0])
            )

    doc_attention, half = None, max(1, group // 2)
    for steps in (range(half), range(half, group)):
        if steps:
            doc_attention, *brought = document_heads(
                spot,
                document_query,
                steps,
                [own_pieces[step] for step in steps],
                [anchors[step] for step in steps],
                doc_attention,
                out_weight if steps[-1] == group - 1 else None,
            )
    (near_weight,) = brought
    blocks = [
        (member ^ member_step) * ring + (turn ^ step) for (member_step, step), _, _ in chunks
    ]
    shares = project(
        joined(*blocks),
        [(array, start) for _, array, start in chunks],
        near_weight,
        row_count,
        unit_heads,
        head_size,
        joined(lax.axis_index("head")),
    )
    question_out = shares[0]
    for step in range(1, head_size):
        question_out = question_out + swapped(shares[step], "head", head_size, step).astype(
            jnp.float32
        )
    return doc_attention, question_out.astype(jnp.bfloat16)


def solution(mesh):
    placed = (
        P("ctx", "head"),
        P("ctx", "head"),
        P("ctx", "head"),
        P(None, "head"),
        P(None, "head"),
        P(None, "head"),
        P("head", "ctx"),
    )
    return jax.shard_map(
        functools.partial(local, mesh.shape["ctx"], mesh.shape["head"]),
        mesh=mesh,
        in_specs=placed,
        out_specs=(P("ctx", "head"), P("head", "ctx")),
        check_vma=False,
    )
```

```python
import functools
import math

import jax
import jax.numpy as jnp
from jax import lax
from jax.experimental import pallas as pl
from jax.experimental.pallas import tpu as pltpu
from jax.sharding import PartitionSpec as P

QUERY_HEADS = 64
KEY_VALUE_HEADS = 8
HEAD_SIZE = 128
GROUP_WIDTH = QUERY_HEADS // KEY_VALUE_HEADS
FACTOR = HEAD_SIZE**-0.5
LOG2E = math.log2(math.e)
NEG_INF = float("-inf")
STAT_ROWS = 16
VMEM = pl.BlockSpec(memory_space=pltpu.VMEM)
ANY = pl.BlockSpec(memory_space=pl.ANY)
SMEM = pl.BlockSpec(memory_space=pltpu.SMEM)
PARAMS = pltpu.CompilerParams(vmem_limit_bytes=32 * 1024 * 1024)


def dot_nt(left, right):
    return lax.dot_general(
        left, right, (((1,), (1,)), ((), ())), preferred_element_type=jnp.float32
    )


def dot_nn(left, right):
    return jnp.dot(left, right, preferred_element_type=jnp.float32)


def with_ones(values):
    return jnp.concatenate([values, jnp.ones_like(values)], axis=1)


def columns(index, width):
    return pl.ds(pl.multiple_of(index * width, width), width)


def in_hbm(values):
    return pltpu.with_memory_space_constraint(values, pltpu.MemorySpace.HBM)


def cut_pieces(place, keys, values, group, question=()):
    token_count = keys.shape[0]

    def kernel(place_ref, keys_ref, values_ref, *refs):
        question_refs, refs = refs[: len(question)], refs[len(question) :]
        pieces, cuts, sems = refs[:group], refs[group:-1], refs[-1]
        pairs = []
        for step, piece in enumerate(pieces):
            cut = columns(place_ref[0] ^ step, HEAD_SIZE)
            for half, source in enumerate((keys_ref, values_ref)):
                pairs.append((source.at[:, cut], piece.at[pl.ds(half * token_count, token_count)]))
        for source, target in zip(question_refs, cuts):
            pairs.append((source.at[:, columns(place_ref[0], target.shape[1])], target))
        copies = [
            pltpu.make_async_copy(source, target, sems.at[i])
            for i, (source, target) in enumerate(pairs)
        ]
        for copy in copies:
            copy.start()
        for copy in copies:
            copy.wait()

    shapes = [jax.ShapeDtypeStruct((2 * token_count, HEAD_SIZE), keys.dtype)] * group + [
        jax.ShapeDtypeStruct((array.shape[0], array.shape[1] // group), array.dtype)
        for array in question
    ]
    return pl.pallas_call(
        kernel,
        out_shape=shapes,
        in_specs=[SMEM] + [ANY] * (2 + len(question)),
        out_specs=[ANY] * len(shapes),
        scratch_shapes=[pltpu.SemaphoreType.DMA((len(shapes) + group,))],
        compiler_params=PARAMS,
        name="cut_pieces",
    )(place, in_hbm(keys), in_hbm(values), *map(in_hbm, question))


def query_copies(place, query_ref, steps, targets, sems):
    return [
        pltpu.make_async_copy(
            query_ref.at[:, columns(place ^ step, target.shape[1])], target, sems.at[i]
        )
        for i, (step, target) in enumerate(zip(steps, targets))
    ]


def query_shapes(query, group, steps):
    shape = (query.shape[0], query.shape[1] // group)
    return [jax.ShapeDtypeStruct(shape, query.dtype)] * len(steps)


def bring_queries(place, query, group, steps, piece):
    def kernel(place_ref, query_ref, piece_ref, *refs):
        copies = query_copies(place_ref[0], query_ref, steps, refs[:-1], refs[-1])
        for copy in copies:
            copy.start()
        for copy in copies:
            copy.wait()

    return pl.pallas_call(
        kernel,
        out_shape=query_shapes(query, group, steps),
        in_specs=[SMEM, ANY, ANY],
        out_specs=[ANY] * len(steps),
        scratch_shapes=[pltpu.SemaphoreType.DMA((len(steps),))],
        compiler_params=PARAMS,
        name="bring_queries",
    )(place, in_hbm(query), piece)


def question_parts(place, query, own_keys, own_values, pieces, ring):
    group = len(pieces)
    token_count = pieces[0].shape[0] // 2
    row_count, key_count = query.shape[0], own_keys.shape[0]
    unit_heads = query.shape[1] // (HEAD_SIZE * ring)
    unit_columns = unit_heads * HEAD_SIZE
    unit_rows = unit_heads * row_count
    out_shape = (unit_rows + STAT_ROWS, HEAD_SIZE)

    def kernel(place_ref, query_ref, own_keys_ref, own_values_ref, *refs):
        piece_refs, outs = refs[:group], refs[group:]
        all_keys = jnp.concatenate([piece[:token_count] for piece in piece_refs], axis=0)
        all_values = with_ones(jnp.concatenate([piece[token_count:] for piece in piece_refs], axis=0))
        own_keys, own_values = own_keys_ref[...], with_ones(own_values_ref[...])
        lanes = lax.broadcasted_iota(jnp.int32, (row_count, HEAD_SIZE), 1)
        stat_ids = lax.broadcasted_iota(jnp.int32, (STAT_ROWS, row_count), 0)
        visible = lax.broadcasted_iota(jnp.int32, (row_count, key_count), 0) >= (
            lax.broadcasted_iota(jnp.int32, (row_count, key_count), 1)
        )
        visible = jnp.concatenate([visible] * unit_heads, axis=0)
        for step, out in enumerate(outs):
            heads = query_ref[:, columns(place_ref[1] ^ step, unit_columns)]
            queries = jnp.concatenate(
                [heads[:, i * HEAD_SIZE : (i + 1) * HEAD_SIZE] for i in range(unit_heads)], axis=0
            )
            scores, values = dot_nt(queries, all_keys), all_values
            if step == 0:
                own_scores = jnp.where(visible, dot_nt(queries, own_keys), NEG_INF)
                scores = jnp.concatenate([scores, own_scores], axis=1)
                values = jnp.concatenate([values, own_values], axis=0)
            top = scores.max(axis=1, keepdims=True) * FACTOR
            top = top.astype(jnp.bfloat16).astype(jnp.float32)
            weights = jnp.exp2(scores * (FACTOR * LOG2E) - top * LOG2E)
            sums = dot_nn(weights.astype(jnp.bfloat16), values)
            out[:unit_rows] = sums[:, :HEAD_SIZE].astype(jnp.bfloat16)
            totals = sums[:, HEAD_SIZE:]
            stats = jnp.zeros((STAT_ROWS, row_count), jnp.float32)
            for i in range(unit_heads):
                rows = slice(i * row_count, (i + 1) * row_count)
                flipped = jnp.where(lanes < HEAD_SIZE // 2, top[rows], totals[rows]).T
                total = flipped[HEAD_SIZE // 2 : HEAD_SIZE // 2 + 1]
                high = total.astype(jnp.bfloat16).astype(jnp.float32)
                for j, value in enumerate((flipped[:1], high, total - high)):
                    stats = jnp.where(stat_ids == 3 * i + j, value, stats)
            out[unit_rows:] = stats.astype(jnp.bfloat16)

    return pl.pallas_call(
        kernel,
        out_shape=[jax.ShapeDtypeStruct(out_shape, jnp.bfloat16)] * ring,
        in_specs=[SMEM] + [VMEM] * (3 + group),
        out_specs=[VMEM] * ring,
        compiler_params=PARAMS,
        name="question_parts",
    )(place, query, own_keys, own_values, *pieces)


def merge_parts(parts, row_count):
    unit_rows = parts[0].shape[0] - STAT_ROWS
    unit_heads = unit_rows // row_count

    def kernel(*refs):
        part_refs, out = refs[:-1], refs[-1]
        stats = [part[unit_rows:].astype(jnp.float32).T for part in part_refs]
        for i in range(unit_heads):
            rows = slice(i * row_count, (i + 1) * row_count)
            tops = [stat[:, 3 * i : 3 * i + 1] for stat in stats]
            totals = [stat[:, 3 * i + 1 : 3 * i + 2] + stat[:, 3 * i + 2 : 3 * i + 3] for stat in stats]
            row_top = functools.reduce(jnp.maximum, tops)
            scales = [jnp.exp(top - row_top) for top in tops]
            total = sum(scale * value for scale, value in zip(scales, totals))
            merged = sum(
                scale * part[rows].astype(jnp.float32) for scale, part in zip(scales, part_refs)
            )
            out[rows] = (merged / total).astype(jnp.bfloat16)

    return pl.pallas_call(
        kernel,
        out_shape=jax.ShapeDtypeStruct((unit_rows, HEAD_SIZE), jnp.bfloat16),
        in_specs=[VMEM] * len(parts),
        out_specs=VMEM,
        compiler_params=PARAMS,
        name="merge_parts",
    )(*parts)


def project(blocks, chunks, weight, row_count, unit_heads, splits, own_split):
    depth, width = unit_heads * HEAD_SIZE, weight.shape[1]
    arrays, spots = [], []
    for array, start in chunks:
        if not any(array is other for other in arrays):
            arrays.append(array)
        spots.append((next(i for i, other in enumerate(arrays) if other is array), start))

    def kernel(blocks_ref, split_ref, weight_ref, *refs):
        array_refs, outs, total_ref = refs[: len(arrays)], refs[len(arrays) : -1], refs[-1]
        total = None
        for at, (which, start) in enumerate(spots):
            rows = jnp.concatenate(
                [
                    array_refs[which][start + i * row_count : start + (i + 1) * row_count]
                    for i in range(unit_heads)
                ],
                axis=1,
            )
            block = weight_ref[pl.ds(pl.multiple_of(blocks_ref[at] * depth, depth), depth)]
            term = dot_nn(rows, block)
            total = term if total is None else total + term
        total_ref[...] = total
        span = row_count // splits
        for step, out in enumerate(outs):
            start = pl.multiple_of((split_ref[0] ^ step) * span, span)
            out[...] = total_ref[pl.ds(start, span)].astype(out.dtype)

    return pl.pallas_call(
        kernel,
        out_shape=[
            jax.ShapeDtypeStruct(
                (row_count // splits, width), jnp.bfloat16 if step else jnp.float32
            )
            for step in range(splits)
        ],
        in_specs=[SMEM, SMEM, VMEM] + [VMEM] * len(arrays),
        out_specs=[VMEM] * splits,
        scratch_shapes=[pltpu.VMEM((row_count, width), jnp.float32)],
        compiler_params=PARAMS,
        name="project",
    )(blocks, own_split, weight, *arrays)


def document_heads(place, query, group, steps, own, anchors, near, ahead, written, weight):
    count = len(steps)
    token_count, total_columns = query.shape
    step_columns = total_columns // group
    scale = FACTOR * LOG2E
    near = list(near)
    own_fetch = () if near else steps
    given = [array for array in (written, weight) if array is not None]

    def kernel(place_ref, query_ref, *refs):
        refs = list(refs)

        def taken(number):
            head = refs[:number]
            del refs[:number]
            return head

        own_refs, anchor_refs, near_refs = taken(count), taken(count), taken(len(near))
        given_refs, (out,) = taken(len(given)), taken(1)
        ahead_refs = taken(len(ahead))
        weight_outs = taken(1 if weight is not None else 0)
        held, sems, weight_sem, fetch_sems, ahead_sems = taken(5)
        if own_fetch:
            (fetched,) = taken(1)
            near_refs = [fetched.at[i] for i in range(count)]
        member = place_ref[0]
        fetches = query_copies(member, query_ref, own_fetch, near_refs, fetch_sems)
        later = query_copies(member, query_ref, ahead, ahead_refs, ahead_sems)
        if weight is not None:
            later.append(pltpu.make_async_copy(given_refs[-1], weight_outs[0], weight_sem))
        for copy in fetches:
            copy.start()
        if not fetches:
            for copy in later:
                copy.start()
        cuts = [columns(member ^ step, step_columns) for step in steps]
        after_anchor = place_ref[1] > 0
        visible = lax.broadcasted_iota(jnp.int32, (token_count, token_count), 0) >= (
            lax.broadcasted_iota(jnp.int32, (token_count, token_count), 1)
        )
        copies = []
        for step in range(count):
            if fetches and step == 0:
                fetches[0].wait()
            if fetches and step == min(1, count - 1):
                for copy in fetches[1:]:
                    copy.wait()
                for copy in later:
                    copy.start()
            pair = (anchor_refs[step], own_refs[step])
            all_keys = jnp.concatenate([ref[:token_count] for ref in pair], axis=0)
            all_values = with_ones(
                jnp.concatenate([ref[token_count : 2 * token_count] for ref in pair], axis=0)
            )
            for head in range(GROUP_WIDTH):
                spot = slice(head * HEAD_SIZE, (head + 1) * HEAD_SIZE)
                scores = dot_nt(near_refs[step][:, spot], all_keys)
                anchor_scores = scores[:, :token_count]
                own_scores = jnp.where(visible, scores[:, token_count:], NEG_INF)
                own_top = own_scores.max(axis=1, keepdims=True)
                anchor_top = anchor_scores.max(axis=1, keepdims=True)
                top = jnp.where(after_anchor, jnp.maximum(own_top, anchor_top), own_top) * scale
                anchor_shift = jnp.where(after_anchor, top, 1e30)
                anchor_exp = jnp.exp2(anchor_scores * scale - anchor_shift).astype(jnp.bfloat16)
                own_exp = jnp.exp2(own_scores * scale - top).astype(jnp.bfloat16)
                mixture = dot_nn(jnp.concatenate([anchor_exp, own_exp], axis=1), all_values)
                held[step, :, spot] = (mixture[:, :HEAD_SIZE] / mixture[:, HEAD_SIZE:]).astype(
                    held.dtype
                )
            copies.append(
                pltpu.make_async_copy(held.at[step], out.at[:, cuts[step]], sems.at[step])
            )
            copies[-1].start()
        for copy in copies + later:
            copy.wait()

    scratch = [
        pltpu.VMEM((count, token_count, step_columns), query.dtype),
        pltpu.SemaphoreType.DMA((count,)),
        pltpu.SemaphoreType.DMA,
        pltpu.SemaphoreType.DMA((count,)),
        pltpu.SemaphoreType.DMA((max(1, len(ahead)),)),
    ]
    if own_fetch:
        scratch.append(pltpu.VMEM((count, token_count, step_columns), query.dtype))
    out_shape = [jax.ShapeDtypeStruct(query.shape, query.dtype)]
    out_shape += query_shapes(query, group, ahead)
    if weight is not None:
        out_shape.append(jax.ShapeDtypeStruct(weight.shape, weight.dtype))
    return pl.pallas_call(
        kernel,
        out_shape=out_shape,
        in_specs=[SMEM, ANY] + [VMEM] * (2 * count + len(near)) + [ANY] * len(given),
        out_specs=[ANY] * len(out_shape),
        input_output_aliases={} if written is None else {2 + 2 * count + len(near): 0},
        scratch_shapes=scratch,
        compiler_params=PARAMS,
        name="document_heads",
    )(place, in_hbm(query), *own, *anchors, *near, *map(in_hbm, given))


def joined(*scalars):
    return jnp.stack([jnp.asarray(scalar, jnp.int32) for scalar in scalars])


def swapped(values, axis, size, step):
    return lax.ppermute(values, axis, [(place, place ^ step) for place in range(size)])


def question_by_reduction(query, keys, values, prompt_keys, prompt_values, weight):
    row_count = query.shape[0]
    kv_total = keys.shape[1] // HEAD_SIZE
    queries = query.reshape(row_count, kv_total, GROUP_WIDTH, HEAD_SIZE)

    def part(key_block, value_block, visible):
        key_block = key_block.reshape(-1, kv_total, HEAD_SIZE)
        value_block = value_block.reshape(-1, kv_total, HEAD_SIZE)
        scores = FACTOR * jnp.einsum(
            "qhgd,khd->hgqk", queries, key_block, preferred_element_type=jnp.float32
        )
        if visible is not None:
            scores = jnp.where(visible, scores, NEG_INF)
        top = scores.max(axis=3, keepdims=True)
        weights = jnp.exp(scores - top)
        sums = jnp.einsum(
            "hgqk,khd->hgqd",
            weights.astype(jnp.bfloat16),
            value_block,
            preferred_element_type=jnp.float32,
        )
        return top, weights.sum(axis=3, keepdims=True), sums

    ids = jnp.arange(row_count, dtype=jnp.int32)
    block_top, block_total, block_sums = part(keys, values, None)
    self_top, self_total, self_sums = part(prompt_keys, prompt_values, ids[:, None] >= ids[None, :])
    row_top = jnp.maximum(lax.pmax(block_top, "ctx"), self_top)
    scale = jnp.exp(block_top - row_top)
    total, sums = lax.psum((block_total * scale, block_sums * scale), "ctx")
    self_scale = jnp.exp(self_top - row_top)
    attention = (sums + self_sums * self_scale) / (total + self_total * self_scale)
    attention = attention.astype(jnp.bfloat16).transpose(2, 0, 1, 3).reshape(row_count, -1)
    return lax.psum_scatter(
        dot_nn(attention, weight).astype(jnp.bfloat16), "head", scatter_dimension=0, tiled=True
    )


def local(
    ctx_size,
    head_size,
    document_query,
    document_keys,
    document_values,
    question_query,
    prompt_keys,
    prompt_values,
    out_weight,
):
    group = document_keys.shape[1] // HEAD_SIZE
    ring = ctx_size // group
    row_count = question_query.shape[0]
    head_total = question_query.shape[1] // HEAD_SIZE
    position = lax.axis_index("ctx")
    member, turn = position % group, position // group
    place = joined(member, turn)

    def in_group(values, step):
        return swapped(values, "ctx", ctx_size, step)

    def in_ring(values, step):
        return swapped(values, "ctx", ctx_size, step * group)

    whole_units = head_total % ctx_size == 0
    question = (question_query, prompt_keys, prompt_values) if whole_units else ()
    cuts = cut_pieces(place, document_keys, document_values, group, question)
    pieces, question = cuts[:group], cuts[group:]
    own_pieces = pieces
    pieces = [pieces[0]] + [in_group(pieces[step], step) for step in range(1, group)]

    half = max(1, group // 2)
    near = ()
    if whole_units:
        near = bring_queries(place, document_query, group, range(half), own_pieces[0])
        pieces, near = lax.optimization_barrier((pieces, near))

    anchor = lax.select_n(member, *pieces) if group > 1 else pieces[0]

    def sent_on(anchor, reach):
        pairs = [
            (turn_at * group + at, (turn_at + reach) * group + at)
            for turn_at in range(0, ring, 2 * reach)
            for at in range(group)
        ]
        arrived = lax.ppermute(anchor, "ctx", pairs)
        return jnp.where(turn % (2 * reach) == reach, arrived, anchor)

    spot = joined(member, position)

    reach = ring // 2
    if not whole_units:
        while reach:
            anchor = sent_on(anchor, reach)
            reach //= 2
        anchors = [anchor] + [in_group(anchor, step) for step in range(1, group)]
        doc_attention = document_heads(
            spot, document_query, group, range(group), own_pieces, anchors, (), (), None, None
        )[0]
        return doc_attention, question_by_reduction(
            question_query, document_keys, document_values, prompt_keys, prompt_values, out_weight
        )

    unit_heads = head_total // ctx_size
    parts = question_parts(place, *question, pieces, ring)
    parts = [parts[0]] + [in_ring(parts[step], step) for step in range(1, ring)]
    while reach > 1:
        anchor = sent_on(anchor, reach)
        reach //= 2
    parts, anchor = lax.optimization_barrier((parts, anchor))
    attention = merge_parts(parts, row_count)
    if reach:
        anchor = sent_on(anchor, reach)
    shards = [attention] + [in_ring(attention, step) for step in range(1, ring)]

    chunks = [((0, step), shards[step], 0) for step in range(ring)]
    both = jnp.concatenate([anchor, attention], axis=0)
    passed = jnp.concatenate(shards[1:], axis=0)
    beside = [in_group(both, step) for step in range(1, group)]
    far = [in_group(passed, step) for step in range(1, group)]
    anchors = [anchor] + beside
    for member_step in range(1, group):
        chunks.append(((member_step, 0), beside[member_step - 1], anchor.shape[0]))
        for step in range(1, ring):
            chunks.append(
                ((member_step, step), far[member_step - 1], (step - 1) * attention.shape[0])
            )

    doc_attention, calls = None, [range(half), range(half, group)][: 2 if group > 1 else 1]
    for steps in calls:
        last = steps[-1] == group - 1
        doc_attention, *brought = document_heads(
            spot,
            document_query,
            group,
            steps,
            [own_pieces[step] for step in steps],
            [anchors[step] for step in steps],
            near,
            () if last else calls[1],
            doc_attention,
            out_weight if last else None,
        )
        near = brought
    (near_weight,) = brought
    blocks = [
        (member ^ member_step) * ring + (turn ^ step) for (member_step, step), _, _ in chunks
    ]
    shares = project(
        joined(*blocks),
        [(array, start) for _, array, start in chunks],
        near_weight,
        row_count,
        unit_heads,
        head_size,
        joined(lax.axis_index("head")),
    )
    question_out = shares[0]
    for step in range(1, head_size):
        question_out = question_out + swapped(shares[step], "head", head_size, step).astype(
            jnp.float32
        )
    return doc_attention, question_out.astype(jnp.bfloat16)


def solution(mesh):
    placed = (
        P("ctx", "head"),
        P("ctx", "head"),
        P("ctx", "head"),
        P(None, "head"),
        P(None, "head"),
        P(None, "head"),
        P("head", "ctx"),
    )
    return jax.shard_map(
        functools.partial(local, mesh.shape["ctx"], mesh.shape["head"]),
        mesh=mesh,
        in_specs=placed,
        out_specs=(P("ctx", "head"), P("head", "ctx")),
        check_vma=False,
    )
```

```python
import functools
import math

import jax
import jax.numpy as jnp
from jax import lax
from jax.experimental import pallas as pl
from jax.experimental.pallas import tpu as pltpu
from jax.sharding import PartitionSpec as P

QUERY_HEADS = 64
KEY_VALUE_HEADS = 8
HEAD_SIZE = 128
GROUP_WIDTH = QUERY_HEADS // KEY_VALUE_HEADS
FACTOR = HEAD_SIZE**-0.5
LOG2E = math.log2(math.e)
NEG_INF = float("-inf")
STAT_ROWS = 16
VMEM = pl.BlockSpec(memory_space=pltpu.VMEM)
ANY = pl.BlockSpec(memory_space=pl.ANY)
SMEM = pl.BlockSpec(memory_space=pltpu.SMEM)
PARAMS = pltpu.CompilerParams(vmem_limit_bytes=32 * 1024 * 1024)


def dot_nt(left, right):
    return lax.dot_general(
        left, right, (((1,), (1,)), ((), ())), preferred_element_type=jnp.float32
    )


def dot_nn(left, right):
    return jnp.dot(left, right, preferred_element_type=jnp.float32)


def with_ones(values):
    return jnp.concatenate([values, jnp.ones_like(values)], axis=1)


def columns(index, width):
    return pl.ds(pl.multiple_of(index * width, width), width)


def in_hbm(values):
    return pltpu.with_memory_space_constraint(values, pltpu.MemorySpace.HBM)


def cut_pieces(place, keys, values, group):
    token_count = keys.shape[0]

    def kernel(place_ref, keys_ref, values_ref, *refs):
        pieces, sems = refs[:-1], refs[-1]
        pairs = []
        for step, piece in enumerate(pieces):
            cut = columns(place_ref[0] ^ step, HEAD_SIZE)
            for half, source in enumerate((keys_ref, values_ref)):
                pairs.append((source.at[:, cut], piece.at[pl.ds(half * token_count, token_count)]))
        copies = [
            pltpu.make_async_copy(source, target, sems.at[i])
            for i, (source, target) in enumerate(pairs)
        ]
        for copy in copies:
            copy.start()
        for copy in copies:
            copy.wait()

    shape = jax.ShapeDtypeStruct((2 * token_count, HEAD_SIZE), keys.dtype)
    return pl.pallas_call(
        kernel,
        out_shape=[shape] * group,
        in_specs=[SMEM, ANY, ANY],
        out_specs=[ANY] * group,
        scratch_shapes=[pltpu.SemaphoreType.DMA((2 * group,))],
        compiler_params=PARAMS,
        name="cut_pieces",
    )(place, in_hbm(keys), in_hbm(values))


def query_copies(place, query_ref, steps, targets, sems):
    return [
        pltpu.make_async_copy(
            query_ref.at[:, columns(place ^ step, target.shape[1])], target, sems.at[i]
        )
        for i, (step, target) in enumerate(zip(steps, targets))
    ]


def query_shapes(query, group, steps):
    shape = (query.shape[0], query.shape[1] // group)
    return [jax.ShapeDtypeStruct(shape, query.dtype)] * len(steps)


def bring_queries(place, query, group, steps, question, piece):
    count = len(steps)

    def kernel(place_ref, query_ref, piece_ref, *refs):
        question_refs, refs = refs[: len(question)], refs[len(question) :]
        targets, sems = refs[:-1], refs[-1]
        copies = query_copies(place_ref[0], query_ref, steps, targets[:count], sems)
        for at, (source, target) in enumerate(zip(question_refs, targets[count:])):
            cut = columns(place_ref[0], target.shape[1])
            copies.append(pltpu.make_async_copy(source.at[:, cut], target, sems.at[count + at]))
        for copy in copies:
            copy.start()
        for copy in copies:
            copy.wait()

    shapes = query_shapes(query, group, steps)
    for array in question:
        shapes.append(
            jax.ShapeDtypeStruct((array.shape[0], array.shape[1] // group), array.dtype)
        )
    return pl.pallas_call(
        kernel,
        out_shape=shapes,
        in_specs=[SMEM, ANY, ANY] + [ANY] * len(question),
        out_specs=[ANY] * len(shapes),
        scratch_shapes=[pltpu.SemaphoreType.DMA((len(shapes),))],
        compiler_params=PARAMS,
        name="bring_queries",
    )(place, in_hbm(query), piece, *map(in_hbm, question))


def question_parts(place, query, own_keys, own_values, pieces, ring):
    group = len(pieces)
    token_count = pieces[0].shape[0] // 2
    row_count, key_count = query.shape[0], own_keys.shape[0]
    unit_heads = query.shape[1] // (HEAD_SIZE * ring)
    unit_columns = unit_heads * HEAD_SIZE
    unit_rows = unit_heads * row_count
    out_shape = (unit_rows + STAT_ROWS, HEAD_SIZE)

    def kernel(place_ref, query_ref, own_keys_ref, own_values_ref, *refs):
        piece_refs, outs = refs[:group], refs[group:]
        all_keys = jnp.concatenate([piece[:token_count] for piece in piece_refs], axis=0)
        all_values = with_ones(jnp.concatenate([piece[token_count:] for piece in piece_refs], axis=0))
        own_keys, own_values = own_keys_ref[...], with_ones(own_values_ref[...])
        lanes = lax.broadcasted_iota(jnp.int32, (row_count, HEAD_SIZE), 1)
        stat_ids = lax.broadcasted_iota(jnp.int32, (STAT_ROWS, row_count), 0)
        visible = lax.broadcasted_iota(jnp.int32, (row_count, key_count), 0) >= (
            lax.broadcasted_iota(jnp.int32, (row_count, key_count), 1)
        )
        visible = jnp.concatenate([visible] * unit_heads, axis=0)
        for step, out in enumerate(outs):
            heads = query_ref[:, columns(place_ref[1] ^ step, unit_columns)]
            queries = jnp.concatenate(
                [heads[:, i * HEAD_SIZE : (i + 1) * HEAD_SIZE] for i in range(unit_heads)], axis=0
            )
            scores, values = dot_nt(queries, all_keys), all_values
            if step == 0:
                own_scores = jnp.where(visible, dot_nt(queries, own_keys), NEG_INF)
                scores = jnp.concatenate([scores, own_scores], axis=1)
                values = jnp.concatenate([values, own_values], axis=0)
            top = scores.max(axis=1, keepdims=True) * FACTOR
            top = top.astype(jnp.bfloat16).astype(jnp.float32)
            weights = jnp.exp2(scores * (FACTOR * LOG2E) - top * LOG2E)
            sums = dot_nn(weights.astype(jnp.bfloat16), values)
            out[:unit_rows] = sums[:, :HEAD_SIZE].astype(jnp.bfloat16)
            totals = sums[:, HEAD_SIZE:]
            stats = jnp.zeros((STAT_ROWS, row_count), jnp.float32)
            for i in range(unit_heads):
                rows = slice(i * row_count, (i + 1) * row_count)
                flipped = jnp.where(lanes < HEAD_SIZE // 2, top[rows], totals[rows]).T
                total = flipped[HEAD_SIZE // 2 : HEAD_SIZE // 2 + 1]
                high = total.astype(jnp.bfloat16).astype(jnp.float32)
                for j, value in enumerate((flipped[:1], high, total - high)):
                    stats = jnp.where(stat_ids == 3 * i + j, value, stats)
            out[unit_rows:] = stats.astype(jnp.bfloat16)

    return pl.pallas_call(
        kernel,
        out_shape=[jax.ShapeDtypeStruct(out_shape, jnp.bfloat16)] * ring,
        in_specs=[SMEM] + [VMEM] * (3 + group),
        out_specs=[VMEM] * ring,
        compiler_params=PARAMS,
        name="question_parts",
    )(place, query, own_keys, own_values, *pieces)


def merge_parts(parts, row_count):
    unit_rows = parts[0].shape[0] - STAT_ROWS
    unit_heads = unit_rows // row_count

    def kernel(*refs):
        part_refs, out = refs[:-1], refs[-1]
        stats = [part[unit_rows:].astype(jnp.float32).T for part in part_refs]
        for i in range(unit_heads):
            rows = slice(i * row_count, (i + 1) * row_count)
            tops = [stat[:, 3 * i : 3 * i + 1] for stat in stats]
            totals = [stat[:, 3 * i + 1 : 3 * i + 2] + stat[:, 3 * i + 2 : 3 * i + 3] for stat in stats]
            row_top = functools.reduce(jnp.maximum, tops)
            scales = [jnp.exp(top - row_top) for top in tops]
            total = sum(scale * value for scale, value in zip(scales, totals))
            merged = sum(
                scale * part[rows].astype(jnp.float32) for scale, part in zip(scales, part_refs)
            )
            out[rows] = (merged / total).astype(jnp.bfloat16)

    return pl.pallas_call(
        kernel,
        out_shape=jax.ShapeDtypeStruct((unit_rows, HEAD_SIZE), jnp.bfloat16),
        in_specs=[VMEM] * len(parts),
        out_specs=VMEM,
        compiler_params=PARAMS,
        name="merge_parts",
    )(*parts)


def project(place, chunks, weight, row_count, unit_heads, ring, splits):
    depth, width = unit_heads * HEAD_SIZE, weight.shape[1]
    arrays, spots = [], []
    for group_step, ring_step, array, start in chunks:
        if not any(array is other for other in arrays):
            arrays.append(array)
        which = next(i for i, other in enumerate(arrays) if other is array)
        spots.append((group_step, ring_step, which, start))

    def kernel(place_ref, weight_ref, *refs):
        array_refs, outs, total_ref = refs[: len(arrays)], refs[len(arrays) : -1], refs[-1]
        total = None
        for group_step, ring_step, which, start in spots:
            unit = (place_ref[0] ^ group_step) * ring + (place_ref[1] ^ ring_step)
            rows = jnp.concatenate(
                [
                    array_refs[which][start + i * row_count : start + (i + 1) * row_count]
                    for i in range(unit_heads)
                ],
                axis=1,
            )
            block = weight_ref[pl.ds(pl.multiple_of(unit * depth, depth), depth)]
            term = dot_nn(rows, block)
            total = term if total is None else total + term
        total_ref[...] = total
        span = row_count // splits
        for step, out in enumerate(outs):
            start = pl.multiple_of((place_ref[2] ^ step) * span, span)
            out[...] = total_ref[pl.ds(start, span)].astype(out.dtype)

    return pl.pallas_call(
        kernel,
        out_shape=[
            jax.ShapeDtypeStruct(
                (row_count // splits, width), jnp.bfloat16 if step else jnp.float32
            )
            for step in range(splits)
        ],
        in_specs=[SMEM, VMEM] + [VMEM] * len(arrays),
        out_specs=[VMEM] * splits,
        scratch_shapes=[pltpu.VMEM((row_count, width), jnp.float32)],
        compiler_params=PARAMS,
        name="project",
    )(place, weight, *arrays)


def document_heads(place, query, group, steps, own, anchors, near, ahead, written, weight):
    count = len(steps)
    token_count, total_columns = query.shape
    step_columns = total_columns // group
    scale = FACTOR * LOG2E
    near = list(near)
    own_fetch = () if near else steps
    given = [array for array in (written, weight) if array is not None]

    def kernel(place_ref, query_ref, *refs):
        refs = list(refs)

        def taken(number):
            head = refs[:number]
            del refs[:number]
            return head

        own_refs, anchor_refs, near_refs = taken(count), taken(count), taken(len(near))
        given_refs, (out,) = taken(len(given)), taken(1)
        ahead_refs = taken(len(ahead))
        weight_outs = taken(1 if weight is not None else 0)
        held, sems, weight_sem, fetch_sems, ahead_sems = taken(5)
        if own_fetch:
            (fetched,) = taken(1)
            near_refs = [fetched.at[i] for i in range(count)]
        member = place_ref[0]
        fetches = query_copies(member, query_ref, own_fetch, near_refs, fetch_sems)
        later = query_copies(member, query_ref, ahead, ahead_refs, ahead_sems)
        if weight is not None:
            later.append(pltpu.make_async_copy(given_refs[-1], weight_outs[0], weight_sem))
        for copy in fetches:
            copy.start()
        if not fetches:
            for copy in later:
                copy.start()
        cuts = [columns(member ^ step, step_columns) for step in steps]
        after_anchor = place_ref[0] + place_ref[1] > 0
        visible = lax.broadcasted_iota(jnp.int32, (token_count, token_count), 0) >= (
            lax.broadcasted_iota(jnp.int32, (token_count, token_count), 1)
        )
        copies = []
        for step in range(count):
            if fetches and step == 0:
                fetches[0].wait()
            if fetches and step == min(1, count - 1):
                for copy in fetches[1:]:
                    copy.wait()
                for copy in later:
                    copy.start()
            pair = (anchor_refs[step], own_refs[step])
            all_keys = jnp.concatenate([ref[:token_count] for ref in pair], axis=0)
            all_values = with_ones(
                jnp.concatenate([ref[token_count : 2 * token_count] for ref in pair], axis=0)
            )
            for head in range(GROUP_WIDTH):
                spot = slice(head * HEAD_SIZE, (head + 1) * HEAD_SIZE)
                scores = dot_nt(near_refs[step][:, spot], all_keys)
                anchor_scores = scores[:, :token_count]
                own_scores = jnp.where(visible, scores[:, token_count:], NEG_INF)
                own_top = own_scores.max(axis=1, keepdims=True)
                anchor_top = anchor_scores.max(axis=1, keepdims=True)
                top = jnp.where(after_anchor, jnp.maximum(own_top, anchor_top), own_top) * scale
                anchor_shift = jnp.where(after_anchor, top, 1e30)
                anchor_exp = jnp.exp2(anchor_scores * scale - anchor_shift).astype(jnp.bfloat16)
                own_exp = jnp.exp2(own_scores * scale - top).astype(jnp.bfloat16)
                mixture = dot_nn(jnp.concatenate([anchor_exp, own_exp], axis=1), all_values)
                held[step, :, spot] = (mixture[:, :HEAD_SIZE] / mixture[:, HEAD_SIZE:]).astype(
                    held.dtype
                )
            copies.append(
                pltpu.make_async_copy(held.at[step], out.at[:, cuts[step]], sems.at[step])
            )
            copies[-1].start()
        for copy in copies + later:
            copy.wait()

    scratch = [
        pltpu.VMEM((count, token_count, step_columns), query.dtype),
        pltpu.SemaphoreType.DMA((count,)),
        pltpu.SemaphoreType.DMA,
        pltpu.SemaphoreType.DMA((count,)),
        pltpu.SemaphoreType.DMA((max(1, len(ahead)),)),
    ]
    if own_fetch:
        scratch.append(pltpu.VMEM((count, token_count, step_columns), query.dtype))
    out_shape = [jax.ShapeDtypeStruct(query.shape, query.dtype)]
    out_shape += query_shapes(query, group, ahead)
    if weight is not None:
        out_shape.append(jax.ShapeDtypeStruct(weight.shape, weight.dtype))
    return pl.pallas_call(
        kernel,
        out_shape=out_shape,
        in_specs=[SMEM, ANY] + [VMEM] * (2 * count + len(near)) + [ANY] * len(given),
        out_specs=[ANY] * len(out_shape),
        input_output_aliases={} if written is None else {2 + 2 * count + len(near): 0},
        scratch_shapes=scratch,
        compiler_params=PARAMS,
        name="document_heads",
    )(place, in_hbm(query), *own, *anchors, *near, *map(in_hbm, given))


def joined(*scalars):
    return jnp.stack([jnp.asarray(scalar, jnp.int32) for scalar in scalars])


def swapped(values, axis, size, step):
    return lax.ppermute(values, axis, [(place, place ^ step) for place in range(size)])


def question_by_reduction(query, keys, values, prompt_keys, prompt_values, weight):
    row_count = query.shape[0]
    kv_total = keys.shape[1] // HEAD_SIZE
    queries = query.reshape(row_count, kv_total, GROUP_WIDTH, HEAD_SIZE)

    def part(key_block, value_block, visible):
        key_block = key_block.reshape(-1, kv_total, HEAD_SIZE)
        value_block = value_block.reshape(-1, kv_total, HEAD_SIZE)
        scores = FACTOR * jnp.einsum(
            "qhgd,khd->hgqk", queries, key_block, preferred_element_type=jnp.float32
        )
        if visible is not None:
            scores = jnp.where(visible, scores, NEG_INF)
        top = scores.max(axis=3, keepdims=True)
        weights = jnp.exp(scores - top)
        sums = jnp.einsum(
            "hgqk,khd->hgqd",
            weights.astype(jnp.bfloat16),
            value_block,
            preferred_element_type=jnp.float32,
        )
        return top, weights.sum(axis=3, keepdims=True), sums

    ids = jnp.arange(row_count, dtype=jnp.int32)
    block_top, block_total, block_sums = part(keys, values, None)
    self_top, self_total, self_sums = part(prompt_keys, prompt_values, ids[:, None] >= ids[None, :])
    row_top = jnp.maximum(lax.pmax(block_top, "ctx"), self_top)
    scale = jnp.exp(block_top - row_top)
    total, sums = lax.psum((block_total * scale, block_sums * scale), "ctx")
    self_scale = jnp.exp(self_top - row_top)
    attention = (sums + self_sums * self_scale) / (total + self_total * self_scale)
    attention = attention.astype(jnp.bfloat16).transpose(2, 0, 1, 3).reshape(row_count, -1)
    return lax.psum_scatter(
        dot_nn(attention, weight).astype(jnp.bfloat16), "head", scatter_dimension=0, tiled=True
    )


def local(
    ctx_size,
    head_size,
    document_query,
    document_keys,
    document_values,
    question_query,
    prompt_keys,
    prompt_values,
    out_weight,
):
    group = document_keys.shape[1] // HEAD_SIZE
    ring = ctx_size // group
    row_count = question_query.shape[0]
    head_total = question_query.shape[1] // HEAD_SIZE
    position = lax.axis_index("ctx")
    member, turn = position % group, position // group
    place = joined(member, turn, lax.axis_index("head"))

    def in_group(values, step):
        return swapped(values, "ctx", ctx_size, step)

    def in_ring(values, step):
        return swapped(values, "ctx", ctx_size, step * group)

    whole_units = head_total % ctx_size == 0
    question = (question_query, prompt_keys, prompt_values) if whole_units else ()
    own_pieces = cut_pieces(place, document_keys, document_values, group)
    pieces = own_pieces
    pieces = [pieces[0]] + [in_group(pieces[step], step) for step in range(1, group)]

    half = max(1, group // 2)
    near = ()
    if whole_units:
        near = bring_queries(place, document_query, group, range(half), question, own_pieces[0])
        pieces, near = lax.optimization_barrier((pieces, near))
        near, question = near[:half], near[half:]

    anchor = lax.select_n(member, *pieces) if group > 1 else pieces[0]

    def sent_on(anchor, reach):
        pairs = [
            (turn_at * group + at, (turn_at + reach) * group + at)
            for turn_at in range(0, ring, 2 * reach)
            for at in range(group)
        ]
        arrived = lax.ppermute(anchor, "ctx", pairs)
        return jnp.where(turn % (2 * reach) == reach, arrived, anchor)

    reach = ring // 2
    if not whole_units:
        while reach:
            anchor = sent_on(anchor, reach)
            reach //= 2
        anchors = [anchor] + [in_group(anchor, step) for step in range(1, group)]
        doc_attention = document_heads(
            place, document_query, group, range(group), own_pieces, anchors, (), (), None, None
        )[0]
        return doc_attention, question_by_reduction(
            question_query, document_keys, document_values, prompt_keys, prompt_values, out_weight
        )

    unit_heads = head_total // ctx_size
    parts = question_parts(place, *question, pieces, ring)
    parts = [parts[0]] + [in_ring(parts[step], step) for step in range(1, ring)]
    while reach > 1:
        anchor = sent_on(anchor, reach)
        reach //= 2
    parts, anchor = lax.optimization_barrier((parts, anchor))
    attention = merge_parts(parts, row_count)
    if reach:
        anchor = sent_on(anchor, reach)
    shards = [attention] + [in_ring(attention, step) for step in range(1, ring)]

    chunks = [(0, step, shards[step], 0) for step in range(ring)]
    both = jnp.concatenate([anchor, attention], axis=0)
    passed = jnp.concatenate(shards[1:], axis=0)
    beside = [in_group(both, step) for step in range(1, group)]
    far = [in_group(passed, step) for step in range(1, group)]
    anchors = [anchor] + beside
    for member_step in range(1, group):
        chunks.append((member_step, 0, beside[member_step - 1], anchor.shape[0]))
        for step in range(1, ring):
            chunks.append(
                (member_step, step, far[member_step - 1], (step - 1) * attention.shape[0])
            )

    doc_attention, calls = None, [range(half), range(half, group)][: 2 if group > 1 else 1]
    for steps in calls:
        last = steps[-1] == group - 1
        doc_attention, *brought = document_heads(
            place,
            document_query,
            group,
            steps,
            [own_pieces[step] for step in steps],
            [anchors[step] for step in steps],
            near,
            () if last else calls[1],
            doc_attention,
            out_weight if last else None,
        )
        near = brought
    (near_weight,) = brought
    shares = project(place, chunks, near_weight, row_count, unit_heads, ring, head_size)
    question_out = shares[0]
    for step in range(1, head_size):
        question_out = question_out + swapped(shares[step], "head", head_size, step).astype(
            jnp.float32
        )
    return doc_attention, question_out.astype(jnp.bfloat16)


def solution(mesh):
    placed = (
        P("ctx", "head"),
        P("ctx", "head"),
        P("ctx", "head"),
        P(None, "head"),
        P(None, "head"),
        P(None, "head"),
        P("head", "ctx"),
    )
    return jax.shard_map(
        functools.partial(local, mesh.shape["ctx"], mesh.shape["head"]),
        mesh=mesh,
        in_specs=placed,
        out_specs=(P("ctx", "head"), P("head", "ctx")),
        check_vma=False,
    )
```

```python
import functools
import math

import jax
import jax.numpy as jnp
from jax import lax
from jax.experimental import pallas as pl
from jax.experimental.pallas import tpu as pltpu
from jax.sharding import PartitionSpec as P

QUERY_HEADS = 64
KEY_VALUE_HEADS = 8
HEAD_SIZE = 128
GROUP_WIDTH = QUERY_HEADS // KEY_VALUE_HEADS
FACTOR = HEAD_SIZE**-0.5
LOG2E = math.log2(math.e)
NEG_INF = float("-inf")
STAT_ROWS = 16
VMEM = pl.BlockSpec(memory_space=pltpu.VMEM)
ANY = pl.BlockSpec(memory_space=pl.ANY)
SMEM = pl.BlockSpec(memory_space=pltpu.SMEM)
PARAMS = pltpu.CompilerParams(vmem_limit_bytes=32 * 1024 * 1024)


def dot_nt(left, right):
    return lax.dot_general(
        left, right, (((1,), (1,)), ((), ())), preferred_element_type=jnp.float32
    )


def dot_nn(left, right):
    return jnp.dot(left, right, preferred_element_type=jnp.float32)


def with_ones(values):
    return jnp.concatenate([values, jnp.ones_like(values)], axis=1)


def columns(index, width):
    return pl.ds(pl.multiple_of(index * width, width), width)


def in_hbm(values):
    return pltpu.with_memory_space_constraint(values, pltpu.MemorySpace.HBM)


def cut_pieces(place, keys, values, group):
    token_count = keys.shape[0]

    def kernel(place_ref, keys_ref, values_ref, *refs):
        pieces, sems = refs[:-1], refs[-1]
        pairs = []
        for step, piece in enumerate(pieces):
            cut = columns(place_ref[0] ^ step, HEAD_SIZE)
            for half, source in enumerate((keys_ref, values_ref)):
                pairs.append((source.at[:, cut], piece.at[pl.ds(half * token_count, token_count)]))
        copies = [
            pltpu.make_async_copy(source, target, sems.at[i])
            for i, (source, target) in enumerate(pairs)
        ]
        for copy in copies:
            copy.start()
        for copy in copies:
            copy.wait()

    shape = jax.ShapeDtypeStruct((2 * token_count, HEAD_SIZE), keys.dtype)
    return pl.pallas_call(
        kernel,
        out_shape=[shape] * group,
        in_specs=[SMEM, ANY, ANY],
        out_specs=[ANY] * group,
        scratch_shapes=[pltpu.SemaphoreType.DMA((2 * group,))],
        compiler_params=PARAMS,
        name="cut_pieces",
    )(place, in_hbm(keys), in_hbm(values))


def query_copies(place, query_ref, steps, targets, sems):
    return [
        pltpu.make_async_copy(
            query_ref.at[:, columns(place ^ step, target.shape[1])], target, sems.at[i]
        )
        for i, (step, target) in enumerate(zip(steps, targets))
    ]


def query_shapes(query, group, steps):
    shape = (query.shape[0], query.shape[1] // group)
    return [jax.ShapeDtypeStruct(shape, query.dtype)] * len(steps)


def bring_queries(place, query, group, steps, question, piece):
    count = len(steps)

    def kernel(place_ref, query_ref, piece_ref, *refs):
        question_refs, refs = refs[: len(question)], refs[len(question) :]
        targets, sems = refs[:-1], refs[-1]
        copies = query_copies(place_ref[0], query_ref, steps, targets[:count], sems)
        for at, (source, target) in enumerate(zip(question_refs, targets[count:])):
            cut = columns(place_ref[0], target.shape[1])
            copies.append(pltpu.make_async_copy(source.at[:, cut], target, sems.at[count + at]))
        for copy in copies:
            copy.start()
        for copy in copies:
            copy.wait()

    shapes = query_shapes(query, group, steps)
    for array in question:
        shapes.append(
            jax.ShapeDtypeStruct((array.shape[0], array.shape[1] // group), array.dtype)
        )
    return pl.pallas_call(
        kernel,
        out_shape=shapes,
        in_specs=[SMEM, ANY, ANY] + [ANY] * len(question),
        out_specs=[ANY] * len(shapes),
        scratch_shapes=[pltpu.SemaphoreType.DMA((len(shapes),))],
        compiler_params=PARAMS,
        name="bring_queries",
    )(place, in_hbm(query), piece, *map(in_hbm, question))


def question_parts(place, query, own_keys, own_values, pieces, ring):
    group = len(pieces)
    token_count = pieces[0].shape[0] // 2
    row_count, key_count = query.shape[0], own_keys.shape[0]
    unit_heads = query.shape[1] // (HEAD_SIZE * ring)
    unit_columns = unit_heads * HEAD_SIZE
    unit_rows = unit_heads * row_count
    out_shape = (unit_rows + STAT_ROWS, HEAD_SIZE)

    def kernel(place_ref, query_ref, own_keys_ref, own_values_ref, *refs):
        piece_refs, outs = refs[:group], refs[group:]
        all_keys = jnp.concatenate([piece[:token_count] for piece in piece_refs], axis=0)
        all_values = with_ones(jnp.concatenate([piece[token_count:] for piece in piece_refs], axis=0))
        own_keys, own_values = own_keys_ref[...], with_ones(own_values_ref[...])
        lanes = lax.broadcasted_iota(jnp.int32, (row_count, HEAD_SIZE), 1)
        stat_ids = lax.broadcasted_iota(jnp.int32, (STAT_ROWS, row_count), 0)
        visible = lax.broadcasted_iota(jnp.int32, (row_count, key_count), 0) >= (
            lax.broadcasted_iota(jnp.int32, (row_count, key_count), 1)
        )
        visible = jnp.concatenate([visible] * unit_heads, axis=0)
        for step, out in enumerate(outs):
            heads = query_ref[:, columns(place_ref[1] ^ step, unit_columns)]
            queries = jnp.concatenate(
                [heads[:, i * HEAD_SIZE : (i + 1) * HEAD_SIZE] for i in range(unit_heads)], axis=0
            )
            scores, values = dot_nt(queries, all_keys), all_values
            if step == 0:
                own_scores = jnp.where(visible, dot_nt(queries, own_keys), NEG_INF)
                scores = jnp.concatenate([scores, own_scores], axis=1)
                values = jnp.concatenate([values, own_values], axis=0)
            top = scores.max(axis=1, keepdims=True) * FACTOR
            top = top.astype(jnp.bfloat16).astype(jnp.float32)
            weights = jnp.exp2(scores * (FACTOR * LOG2E) - top * LOG2E)
            sums = dot_nn(weights.astype(jnp.bfloat16), values)
            out[:unit_rows] = sums[:, :HEAD_SIZE].astype(jnp.bfloat16)
            totals = sums[:, HEAD_SIZE:]
            stats = jnp.zeros((STAT_ROWS, row_count), jnp.float32)
            for i in range(unit_heads):
                rows = slice(i * row_count, (i + 1) * row_count)
                flipped = jnp.where(lanes < HEAD_SIZE // 2, top[rows], totals[rows]).T
                total = flipped[HEAD_SIZE // 2 : HEAD_SIZE // 2 + 1]
                high = total.astype(jnp.bfloat16).astype(jnp.float32)
                for j, value in enumerate((flipped[:1], high, total - high)):
                    stats = jnp.where(stat_ids == 3 * i + j, value, stats)
            out[unit_rows:] = stats.astype(jnp.bfloat16)

    return pl.pallas_call(
        kernel,
        out_shape=[jax.ShapeDtypeStruct(out_shape, jnp.bfloat16)] * ring,
        in_specs=[SMEM] + [VMEM] * (3 + group),
        out_specs=[VMEM] * ring,
        compiler_params=PARAMS,
        name="question_parts",
    )(place, query, own_keys, own_values, *pieces)


def merge_parts(parts, row_count):
    unit_rows = parts[0].shape[0] - STAT_ROWS
    unit_heads = unit_rows // row_count

    def kernel(*refs):
        part_refs, out = refs[:-1], refs[-1]
        stats = [part[unit_rows:].astype(jnp.float32).T for part in part_refs]
        for i in range(unit_heads):
            rows = slice(i * row_count, (i + 1) * row_count)
            tops = [stat[:, 3 * i : 3 * i + 1] for stat in stats]
            totals = [stat[:, 3 * i + 1 : 3 * i + 2] + stat[:, 3 * i + 2 : 3 * i + 3] for stat in stats]
            row_top = functools.reduce(jnp.maximum, tops)
            scales = [jnp.exp(top - row_top) for top in tops]
            total = sum(scale * value for scale, value in zip(scales, totals))
            merged = sum(
                scale * part[rows].astype(jnp.float32) for scale, part in zip(scales, part_refs)
            )
            out[rows] = (merged / total).astype(jnp.bfloat16)

    return pl.pallas_call(
        kernel,
        out_shape=jax.ShapeDtypeStruct((unit_rows, HEAD_SIZE), jnp.bfloat16),
        in_specs=[VMEM] * len(parts),
        out_specs=VMEM,
        compiler_params=PARAMS,
        name="merge_parts",
    )(*parts)


def project(place, chunks, weight, row_count, unit_heads, ring, splits):
    depth, width = unit_heads * HEAD_SIZE, weight.shape[1]
    arrays, spots = [], []
    for group_step, ring_step, array, start in chunks:
        if not any(array is other for other in arrays):
            arrays.append(array)
        which = next(i for i, other in enumerate(arrays) if other is array)
        spots.append((group_step, ring_step, which, start))

    def kernel(place_ref, weight_ref, *refs):
        array_refs, outs, total_ref = refs[: len(arrays)], refs[len(arrays) : -1], refs[-1]
        total = None
        for group_step, ring_step, which, start in spots:
            unit = (place_ref[0] ^ group_step) * ring + (place_ref[1] ^ ring_step)
            rows = jnp.concatenate(
                [
                    array_refs[which][start + i * row_count : start + (i + 1) * row_count]
                    for i in range(unit_heads)
                ],
                axis=1,
            )
            block = weight_ref[pl.ds(pl.multiple_of(unit * depth, depth), depth)]
            term = dot_nn(rows, block)
            total = term if total is None else total + term
        total_ref[...] = total
        span = row_count // splits
        for step, out in enumerate(outs):
            start = pl.multiple_of((place_ref[2] ^ step) * span, span)
            out[...] = total_ref[pl.ds(start, span)].astype(out.dtype)

    return pl.pallas_call(
        kernel,
        out_shape=[
            jax.ShapeDtypeStruct(
                (row_count // splits, width), jnp.bfloat16 if step else jnp.float32
            )
            for step in range(splits)
        ],
        in_specs=[SMEM, VMEM] + [VMEM] * len(arrays),
        out_specs=[VMEM] * splits,
        scratch_shapes=[pltpu.VMEM((row_count, width), jnp.float32)],
        compiler_params=PARAMS,
        name="project",
    )(place, weight, *arrays)


def document_heads(place, query, group, steps, own, anchors, near, ahead, written, weight):
    count = len(steps)
    token_count, total_columns = query.shape
    step_columns = total_columns // group
    scale = FACTOR * LOG2E
    near = list(near)
    own_fetch = () if near else steps
    given = [array for array in (written, weight) if array is not None]

    def kernel(place_ref, query_ref, *refs):
        refs = list(refs)

        def taken(number):
            head = refs[:number]
            del refs[:number]
            return head

        own_refs, anchor_refs, near_refs = taken(count), taken(count), taken(len(near))
        given_refs, (out,) = taken(len(given)), taken(1)
        ahead_refs = taken(len(ahead))
        weight_outs = taken(1 if weight is not None else 0)
        held, sems, weight_sem, fetch_sems, ahead_sems = taken(5)
        if own_fetch:
            (fetched,) = taken(1)
            near_refs = [fetched.at[i] for i in range(count)]
        member = place_ref[0]
        fetches = query_copies(member, query_ref, own_fetch, near_refs, fetch_sems)
        later = query_copies(member, query_ref, ahead, ahead_refs, ahead_sems)
        if weight is not None:
            later.append(pltpu.make_async_copy(given_refs[-1], weight_outs[0], weight_sem))
        for copy in fetches:
            copy.start()
        if not fetches:
            for copy in later:
                copy.start()
        cuts = [columns(member ^ step, step_columns) for step in steps]
        after_anchor = place_ref[0] + place_ref[1] > 0
        visible = lax.broadcasted_iota(jnp.int32, (token_count, token_count), 0) >= (
            lax.broadcasted_iota(jnp.int32, (token_count, token_count), 1)
        )
        copies = []
        for step in range(count):
            if fetches and step == 0:
                fetches[0].wait()
            if fetches and step == min(1, count - 1):
                for copy in fetches[1:]:
                    copy.wait()
                for copy in later:
                    copy.start()
            pair = (anchor_refs[step], own_refs[step])
            anchor_keys, own_keys = (ref[:token_count] for ref in pair)
            anchor_values, own_values = (
                with_ones(ref[token_count : 2 * token_count]) for ref in pair
            )
            for head in range(GROUP_WIDTH):
                spot = slice(head * HEAD_SIZE, (head + 1) * HEAD_SIZE)
                queries = near_refs[step][:, spot]
                anchor_scores = dot_nt(queries, anchor_keys)
                own_scores = jnp.where(visible, dot_nt(queries, own_keys), NEG_INF)
                own_top = own_scores.max(axis=1, keepdims=True)
                anchor_top = anchor_scores.max(axis=1, keepdims=True)
                top = jnp.where(after_anchor, jnp.maximum(own_top, anchor_top), own_top) * scale
                anchor_shift = jnp.where(after_anchor, top, 1e30)
                anchor_exp = jnp.exp2(anchor_scores * scale - anchor_shift).astype(jnp.bfloat16)
                own_exp = jnp.exp2(own_scores * scale - top).astype(jnp.bfloat16)
                mixture = dot_nn(anchor_exp, anchor_values) + dot_nn(own_exp, own_values)
                held[step, :, spot] = (mixture[:, :HEAD_SIZE] / mixture[:, HEAD_SIZE:]).astype(
                    held.dtype
                )
            copies.append(
                pltpu.make_async_copy(held.at[step], out.at[:, cuts[step]], sems.at[step])
            )
            copies[-1].start()
        for copy in copies + later:
            copy.wait()

    scratch = [
        pltpu.VMEM((count, token_count, step_columns), query.dtype),
        pltpu.SemaphoreType.DMA((count,)),
        pltpu.SemaphoreType.DMA,
        pltpu.SemaphoreType.DMA((count,)),
        pltpu.SemaphoreType.DMA((max(1, len(ahead)),)),
    ]
    if own_fetch:
        scratch.append(pltpu.VMEM((count, token_count, step_columns), query.dtype))
    out_shape = [jax.ShapeDtypeStruct(query.shape, query.dtype)]
    out_shape += query_shapes(query, group, ahead)
    if weight is not None:
        out_shape.append(jax.ShapeDtypeStruct(weight.shape, weight.dtype))
    return pl.pallas_call(
        kernel,
        out_shape=out_shape,
        in_specs=[SMEM, ANY] + [VMEM] * (2 * count + len(near)) + [ANY] * len(given),
        out_specs=[ANY] * len(out_shape),
        input_output_aliases={} if written is None else {2 + 2 * count + len(near): 0},
        scratch_shapes=scratch,
        compiler_params=PARAMS,
        name="document_heads",
    )(place, in_hbm(query), *own, *anchors, *near, *map(in_hbm, given))


def joined(*scalars):
    return jnp.stack([jnp.asarray(scalar, jnp.int32) for scalar in scalars])


def swapped(values, axis, size, step):
    return lax.ppermute(values, axis, [(place, place ^ step) for place in range(size)])


def question_by_reduction(query, keys, values, prompt_keys, prompt_values, weight):
    row_count = query.shape[0]
    kv_total = keys.shape[1] // HEAD_SIZE
    queries = query.reshape(row_count, kv_total, GROUP_WIDTH, HEAD_SIZE)

    def part(key_block, value_block, visible):
        key_block = key_block.reshape(-1, kv_total, HEAD_SIZE)
        value_block = value_block.reshape(-1, kv_total, HEAD_SIZE)
        scores = FACTOR * jnp.einsum(
            "qhgd,khd->hgqk", queries, key_block, preferred_element_type=jnp.float32
        )
        if visible is not None:
            scores = jnp.where(visible, scores, NEG_INF)
        top = scores.max(axis=3, keepdims=True)
        weights = jnp.exp(scores - top)
        sums = jnp.einsum(
            "hgqk,khd->hgqd",
            weights.astype(jnp.bfloat16),
            value_block,
            preferred_element_type=jnp.float32,
        )
        return top, weights.sum(axis=3, keepdims=True), sums

    ids = jnp.arange(row_count, dtype=jnp.int32)
    block_top, block_total, block_sums = part(keys, values, None)
    self_top, self_total, self_sums = part(prompt_keys, prompt_values, ids[:, None] >= ids[None, :])
    row_top = jnp.maximum(lax.pmax(block_top, "ctx"), self_top)
    scale = jnp.exp(block_top - row_top)
    total, sums = lax.psum((block_total * scale, block_sums * scale), "ctx")
    self_scale = jnp.exp(self_top - row_top)
    attention = (sums + self_sums * self_scale) / (total + self_total * self_scale)
    attention = attention.astype(jnp.bfloat16).transpose(2, 0, 1, 3).reshape(row_count, -1)
    return lax.psum_scatter(
        dot_nn(attention, weight).astype(jnp.bfloat16), "head", scatter_dimension=0, tiled=True
    )


def local(
    ctx_size,
    head_size,
    document_query,
    document_keys,
    document_values,
    question_query,
    prompt_keys,
    prompt_values,
    out_weight,
):
    group = document_keys.shape[1] // HEAD_SIZE
    ring = ctx_size // group
    row_count = question_query.shape[0]
    head_total = question_query.shape[1] // HEAD_SIZE
    position = lax.axis_index("ctx")
    member, turn = position % group, position // group
    place = joined(member, turn, lax.axis_index("head"))

    def in_group(values, step):
        return swapped(values, "ctx", ctx_size, step)

    def in_ring(values, step):
        return swapped(values, "ctx", ctx_size, step * group)

    whole_units = head_total % ctx_size == 0
    question = (question_query, prompt_keys, prompt_values) if whole_units else ()
    own_pieces = cut_pieces(place, document_keys, document_values, group)
    pieces = own_pieces
    pieces = [pieces[0]] + [in_group(pieces[step], step) for step in range(1, group)]

    half = max(1, group // 2)
    near = ()
    if whole_units:
        near = bring_queries(place, document_query, group, range(half), question, own_pieces[0])
        pieces, near = lax.optimization_barrier((pieces, near))
        near, question = near[:half], near[half:]

    anchor = lax.select_n(member, *pieces) if group > 1 else pieces[0]

    def sent_on(anchor, reach):
        pairs = [
            (turn_at * group + at, (turn_at + reach) * group + at)
            for turn_at in range(0, ring, 2 * reach)
            for at in range(group)
        ]
        arrived = lax.ppermute(anchor, "ctx", pairs)
        return jnp.where(turn % (2 * reach) == reach, arrived, anchor)

    reach = ring // 2
    if not whole_units:
        while reach:
            anchor = sent_on(anchor, reach)
            reach //= 2
        anchors = [anchor] + [in_group(anchor, step) for step in range(1, group)]
        doc_attention = document_heads(
            place, document_query, group, range(group), own_pieces, anchors, (), (), None, None
        )[0]
        return doc_attention, question_by_reduction(
            question_query, document_keys, document_values, prompt_keys, prompt_values, out_weight
        )

    unit_heads = head_total // ctx_size
    parts = question_parts(place, *question, pieces, ring)
    parts = [parts[0]] + [in_ring(parts[step], step) for step in range(1, ring)]
    while reach > 1:
        anchor = sent_on(anchor, reach)
        reach //= 2
    parts, anchor = lax.optimization_barrier((parts, anchor))
    attention = merge_parts(parts, row_count)
    if reach:
        anchor = sent_on(anchor, reach)
    shards = [attention] + [in_ring(attention, step) for step in range(1, ring)]

    chunks = [(0, step, shards[step], 0) for step in range(ring)]
    both = jnp.concatenate([anchor, attention], axis=0)
    passed = jnp.concatenate(shards[1:], axis=0)
    beside = [in_group(both, step) for step in range(1, group)]
    far = [in_group(passed, step) for step in range(1, group)]
    anchors = [anchor] + beside
    for member_step in range(1, group):
        chunks.append((member_step, 0, beside[member_step - 1], anchor.shape[0]))
        for step in range(1, ring):
            chunks.append(
                (member_step, step, far[member_step - 1], (step - 1) * attention.shape[0])
            )

    doc_attention, calls = None, [range(half), range(half, group)][: 2 if group > 1 else 1]
    for steps in calls:
        last = steps[-1] == group - 1
        doc_attention, *brought = document_heads(
            place,
            document_query,
            group,
            steps,
            [own_pieces[step] for step in steps],
            [anchors[step] for step in steps],
            near,
            () if last else calls[1],
            doc_attention,
            out_weight if last else None,
        )
        near = brought
    (near_weight,) = brought
    shares = project(place, chunks, near_weight, row_count, unit_heads, ring, head_size)
    question_out = shares[0]
    for step in range(1, head_size):
        question_out = question_out + swapped(shares[step], "head", head_size, step).astype(
            jnp.float32
        )
    return doc_attention, question_out.astype(jnp.bfloat16)


def solution(mesh):
    placed = (
        P("ctx", "head"),
        P("ctx", "head"),
        P("ctx", "head"),
        P(None, "head"),
        P(None, "head"),
        P(None, "head"),
        P("head", "ctx"),
    )
    return jax.shard_map(
        functools.partial(local, mesh.shape["ctx"], mesh.shape["head"]),
        mesh=mesh,
        in_specs=placed,
        out_specs=(P("ctx", "head"), P("head", "ctx")),
        check_vma=False,
    )
```

```python
import functools
import math

import jax
import jax.numpy as jnp
from jax import lax
from jax.experimental import pallas as pl
from jax.experimental.pallas import tpu as pltpu
from jax.sharding import PartitionSpec as P

QUERY_HEADS = 64
KEY_VALUE_HEADS = 8
HEAD_SIZE = 128
GROUP_WIDTH = QUERY_HEADS // KEY_VALUE_HEADS
FACTOR = HEAD_SIZE**-0.5
LOG2E = math.log2(math.e)
NEG_INF = float("-inf")
STAT_ROWS = 16
VMEM = pl.BlockSpec(memory_space=pltpu.VMEM)
ANY = pl.BlockSpec(memory_space=pl.ANY)
SMEM = pl.BlockSpec(memory_space=pltpu.SMEM)
PARAMS = pltpu.CompilerParams(vmem_limit_bytes=32 * 1024 * 1024)


def dot_nt(left, right):
    return lax.dot_general(
        left, right, (((1,), (1,)), ((), ())), preferred_element_type=jnp.float32
    )


def dot_nn(left, right):
    return jnp.dot(left, right, preferred_element_type=jnp.float32)


def with_ones(values):
    return jnp.concatenate([values, jnp.ones_like(values)], axis=1)


def columns(index, width):
    return pl.ds(pl.multiple_of(index * width, width), width)


def in_hbm(values):
    return pltpu.with_memory_space_constraint(values, pltpu.MemorySpace.HBM)


def cut_pieces(place, keys, values, steps):
    token_count = keys.shape[0]

    def kernel(place_ref, keys_ref, values_ref, *refs):
        pieces, sems = refs[:-1], refs[-1]
        pairs = []
        for step, piece in zip(steps, pieces):
            cut = columns(place_ref[0] ^ step, HEAD_SIZE)
            for half, source in enumerate((keys_ref, values_ref)):
                pairs.append((source.at[:, cut], piece.at[pl.ds(half * token_count, token_count)]))
        copies = [
            pltpu.make_async_copy(source, target, sems.at[i])
            for i, (source, target) in enumerate(pairs)
        ]
        for copy in copies:
            copy.start()
        for copy in copies:
            copy.wait()

    shape = jax.ShapeDtypeStruct((2 * token_count, HEAD_SIZE), keys.dtype)
    return pl.pallas_call(
        kernel,
        out_shape=[shape] * len(steps),
        in_specs=[SMEM, ANY, ANY],
        out_specs=[ANY] * len(steps),
        scratch_shapes=[pltpu.SemaphoreType.DMA((2 * len(steps),))],
        compiler_params=PARAMS,
        name="cut_pieces",
    )(place, in_hbm(keys), in_hbm(values))


def query_copies(place, query_ref, steps, targets, sems):
    return [
        pltpu.make_async_copy(
            query_ref.at[:, columns(place ^ step, target.shape[1])], target, sems.at[i]
        )
        for i, (step, target) in enumerate(zip(steps, targets))
    ]


def query_shapes(query, group, steps):
    shape = (query.shape[0], query.shape[1] // group)
    return [jax.ShapeDtypeStruct(shape, query.dtype)] * len(steps)


def bring_queries(place, query, group, steps, question, piece, keys, values):
    count = len(steps)

    def kernel(place_ref, query_ref, piece_ref, keys_ref, values_ref, *refs):
        question_refs, refs = refs[: len(question)], refs[len(question) :]
        targets, own, sems = refs[:-2], refs[-2], refs[-1]
        copies = query_copies(place_ref[0], query_ref, steps, targets[:count], sems)
        for at, (source, target) in enumerate(zip(question_refs, targets[count:])):
            cut = columns(place_ref[0], target.shape[1])
            copies.append(pltpu.make_async_copy(source.at[:, cut], target, sems.at[count + at]))
        rows = keys.shape[0]
        for half, source in enumerate((keys_ref, values_ref)):
            copies.append(
                pltpu.make_async_copy(
                    source.at[:, columns(place_ref[0], HEAD_SIZE)],
                    own.at[pl.ds(half * rows, rows)],
                    sems.at[count + len(question) + half],
                )
            )
        for copy in copies:
            copy.start()
        for copy in copies:
            copy.wait()

    shapes = query_shapes(query, group, steps)
    for array in question:
        shapes.append(
            jax.ShapeDtypeStruct((array.shape[0], array.shape[1] // group), array.dtype)
        )
    shapes.append(jax.ShapeDtypeStruct(piece.shape, piece.dtype))
    return pl.pallas_call(
        kernel,
        out_shape=shapes,
        in_specs=[SMEM, ANY, ANY, ANY, ANY] + [ANY] * len(question),
        out_specs=[ANY] * len(shapes),
        scratch_shapes=[pltpu.SemaphoreType.DMA((len(shapes) + 1,))],
        compiler_params=PARAMS,
        name="bring_queries",
    )(place, in_hbm(query), piece, in_hbm(keys), in_hbm(values), *map(in_hbm, question))


def question_parts(place, query, own_keys, own_values, pieces, ring):
    group = len(pieces)
    token_count = pieces[0].shape[0] // 2
    row_count, key_count = query.shape[0], own_keys.shape[0]
    unit_heads = query.shape[1] // (HEAD_SIZE * ring)
    unit_columns = unit_heads * HEAD_SIZE
    unit_rows = unit_heads * row_count
    out_shape = (unit_rows + STAT_ROWS, HEAD_SIZE)

    def kernel(place_ref, query_ref, own_keys_ref, own_values_ref, *refs):
        piece_refs, outs = refs[:group], refs[group:]
        all_keys = jnp.concatenate([piece[:token_count] for piece in piece_refs], axis=0)
        all_values = with_ones(jnp.concatenate([piece[token_count:] for piece in piece_refs], axis=0))
        own_keys, own_values = own_keys_ref[...], with_ones(own_values_ref[...])
        lanes = lax.broadcasted_iota(jnp.int32, (row_count, HEAD_SIZE), 1)
        stat_ids = lax.broadcasted_iota(jnp.int32, (STAT_ROWS, row_count), 0)
        visible = lax.broadcasted_iota(jnp.int32, (row_count, key_count), 0) >= (
            lax.broadcasted_iota(jnp.int32, (row_count, key_count), 1)
        )
        visible = jnp.concatenate([visible] * unit_heads, axis=0)
        for step, out in enumerate(outs):
            heads = query_ref[:, columns(place_ref[1] ^ step, unit_columns)]
            queries = jnp.concatenate(
                [heads[:, i * HEAD_SIZE : (i + 1) * HEAD_SIZE] for i in range(unit_heads)], axis=0
            )
            scores, values = dot_nt(queries, all_keys), all_values
            if step == 0:
                own_scores = jnp.where(visible, dot_nt(queries, own_keys), NEG_INF)
                scores = jnp.concatenate([scores, own_scores], axis=1)
                values = jnp.concatenate([values, own_values], axis=0)
            top = scores.max(axis=1, keepdims=True) * FACTOR
            top = top.astype(jnp.bfloat16).astype(jnp.float32)
            weights = jnp.exp2(scores * (FACTOR * LOG2E) - top * LOG2E)
            sums = dot_nn(weights.astype(jnp.bfloat16), values)
            out[:unit_rows] = sums[:, :HEAD_SIZE].astype(jnp.bfloat16)
            totals = sums[:, HEAD_SIZE:]
            stats = jnp.zeros((STAT_ROWS, row_count), jnp.float32)
            for i in range(unit_heads):
                rows = slice(i * row_count, (i + 1) * row_count)
                flipped = jnp.where(lanes < HEAD_SIZE // 2, top[rows], totals[rows]).T
                total = flipped[HEAD_SIZE // 2 : HEAD_SIZE // 2 + 1]
                high = total.astype(jnp.bfloat16).astype(jnp.float32)
                for j, value in enumerate((flipped[:1], high, total - high)):
                    stats = jnp.where(stat_ids == 3 * i + j, value, stats)
            out[unit_rows:] = stats.astype(jnp.bfloat16)

    return pl.pallas_call(
        kernel,
        out_shape=[jax.ShapeDtypeStruct(out_shape, jnp.bfloat16)] * ring,
        in_specs=[SMEM] + [VMEM] * (3 + group),
        out_specs=[VMEM] * ring,
        compiler_params=PARAMS,
        name="question_parts",
    )(place, query, own_keys, own_values, *pieces)


def merge_parts(parts, row_count):
    unit_rows = parts[0].shape[0] - STAT_ROWS
    unit_heads = unit_rows // row_count

    def kernel(*refs):
        part_refs, out = refs[:-1], refs[-1]
        stats = [part[unit_rows:].astype(jnp.float32).T for part in part_refs]
        for i in range(unit_heads):
            rows = slice(i * row_count, (i + 1) * row_count)
            tops = [stat[:, 3 * i : 3 * i + 1] for stat in stats]
            totals = [stat[:, 3 * i + 1 : 3 * i + 2] + stat[:, 3 * i + 2 : 3 * i + 3] for stat in stats]
            row_top = functools.reduce(jnp.maximum, tops)
            scales = [jnp.exp(top - row_top) for top in tops]
            total = sum(scale * value for scale, value in zip(scales, totals))
            merged = sum(
                scale * part[rows].astype(jnp.float32) for scale, part in zip(scales, part_refs)
            )
            out[rows] = (merged / total).astype(jnp.bfloat16)

    return pl.pallas_call(
        kernel,
        out_shape=jax.ShapeDtypeStruct((unit_rows, HEAD_SIZE), jnp.bfloat16),
        in_specs=[VMEM] * len(parts),
        out_specs=VMEM,
        compiler_params=PARAMS,
        name="merge_parts",
    )(*parts)


def project(place, chunks, weight, row_count, unit_heads, ring, splits):
    depth, width = unit_heads * HEAD_SIZE, weight.shape[1]
    arrays, spots = [], []
    for group_step, ring_step, array, start in chunks:
        if not any(array is other for other in arrays):
            arrays.append(array)
        which = next(i for i, other in enumerate(arrays) if other is array)
        spots.append((group_step, ring_step, which, start))

    def kernel(place_ref, weight_ref, *refs):
        array_refs, outs, total_ref = refs[: len(arrays)], refs[len(arrays) : -1], refs[-1]
        total = None
        for group_step, ring_step, which, start in spots:
            unit = (place_ref[0] ^ group_step) * ring + (place_ref[1] ^ ring_step)
            rows = jnp.concatenate(
                [
                    array_refs[which][start + i * row_count : start + (i + 1) * row_count]
                    for i in range(unit_heads)
                ],
                axis=1,
            )
            block = weight_ref[pl.ds(pl.multiple_of(unit * depth, depth), depth)]
            term = dot_nn(rows, block)
            total = term if total is None else total + term
        total_ref[...] = total
        span = row_count // splits
        for step, out in enumerate(outs):
            start = pl.multiple_of((place_ref[2] ^ step) * span, span)
            out[...] = total_ref[pl.ds(start, span)].astype(out.dtype)

    return pl.pallas_call(
        kernel,
        out_shape=[
            jax.ShapeDtypeStruct(
                (row_count // splits, width), jnp.bfloat16 if step else jnp.float32
            )
            for step in range(splits)
        ],
        in_specs=[SMEM, VMEM] + [VMEM] * len(arrays),
        out_specs=[VMEM] * splits,
        scratch_shapes=[pltpu.VMEM((row_count, width), jnp.float32)],
        compiler_params=PARAMS,
        name="project",
    )(place, weight, *arrays)


def document_heads(place, query, group, steps, own, anchors, near, ahead, written, weight):
    count = len(steps)
    token_count, total_columns = query.shape
    step_columns = total_columns // group
    scale = FACTOR * LOG2E
    near = list(near)
    own_fetch = () if near else steps
    given = [array for array in (written, weight) if array is not None]

    def kernel(place_ref, query_ref, *refs):
        refs = list(refs)

        def taken(number):
            head = refs[:number]
            del refs[:number]
            return head

        own_refs, anchor_refs, near_refs = taken(count), taken(count), taken(len(near))
        given_refs, (out,) = taken(len(given)), taken(1)
        ahead_refs = taken(len(ahead))
        weight_outs = taken(1 if weight is not None else 0)
        held, sems, weight_sem, fetch_sems, ahead_sems = taken(5)
        if own_fetch:
            (fetched,) = taken(1)
            near_refs = [fetched.at[i] for i in range(count)]
        member = place_ref[0]
        fetches = query_copies(member, query_ref, own_fetch, near_refs, fetch_sems)
        later = query_copies(member, query_ref, ahead, ahead_refs, ahead_sems)
        if weight is not None:
            later.append(pltpu.make_async_copy(given_refs[-1], weight_outs[0], weight_sem))
        for copy in fetches:
            copy.start()
        if not fetches:
            for copy in later:
                copy.start()
        cuts = [columns(member ^ step, step_columns) for step in steps]
        after_anchor = place_ref[0] + place_ref[1] > 0
        visible = lax.broadcasted_iota(jnp.int32, (token_count, token_count), 0) >= (
            lax.broadcasted_iota(jnp.int32, (token_count, token_count), 1)
        )
        copies = []
        for step in range(count):
            if fetches and step == 0:
                fetches[0].wait()
            if fetches and step == min(1, count - 1):
                for copy in fetches[1:]:
                    copy.wait()
                for copy in later:
                    copy.start()
            pair = (anchor_refs[step], own_refs[step])
            anchor_keys, own_keys = (ref[:token_count] for ref in pair)
            anchor_values, own_values = (
                with_ones(ref[token_count : 2 * token_count]) for ref in pair
            )
            for head in range(GROUP_WIDTH):
                spot = slice(head * HEAD_SIZE, (head + 1) * HEAD_SIZE)
                queries = near_refs[step][:, spot]
                anchor_scores = dot_nt(queries, anchor_keys)
                own_scores = jnp.where(visible, dot_nt(queries, own_keys), NEG_INF)
                own_top = own_scores.max(axis=1, keepdims=True)
                anchor_top = anchor_scores.max(axis=1, keepdims=True)
                top = jnp.where(after_anchor, jnp.maximum(own_top, anchor_top), own_top) * scale
                anchor_shift = jnp.where(after_anchor, top, 1e30)
                anchor_exp = jnp.exp2(anchor_scores * scale - anchor_shift).astype(jnp.bfloat16)
                own_exp = jnp.exp2(own_scores * scale - top).astype(jnp.bfloat16)
                mixture = dot_nn(anchor_exp, anchor_values) + dot_nn(own_exp, own_values)
                held[step, :, spot] = (mixture[:, :HEAD_SIZE] / mixture[:, HEAD_SIZE:]).astype(
                    held.dtype
                )
            copies.append(
                pltpu.make_async_copy(held.at[step], out.at[:, cuts[step]], sems.at[step])
            )
            copies[-1].start()
        for copy in copies + later:
            copy.wait()

    scratch = [
        pltpu.VMEM((count, token_count, step_columns), query.dtype),
        pltpu.SemaphoreType.DMA((count,)),
        pltpu.SemaphoreType.DMA,
        pltpu.SemaphoreType.DMA((count,)),
        pltpu.SemaphoreType.DMA((max(1, len(ahead)),)),
    ]
    if own_fetch:
        scratch.append(pltpu.VMEM((count, token_count, step_columns), query.dtype))
    out_shape = [jax.ShapeDtypeStruct(query.shape, query.dtype)]
    out_shape += query_shapes(query, group, ahead)
    if weight is not None:
        out_shape.append(jax.ShapeDtypeStruct(weight.shape, weight.dtype))
    return pl.pallas_call(
        kernel,
        out_shape=out_shape,
        in_specs=[SMEM, ANY] + [VMEM] * (2 * count + len(near)) + [ANY] * len(given),
        out_specs=[ANY] * len(out_shape),
        input_output_aliases={} if written is None else {2 + 2 * count + len(near): 0},
        scratch_shapes=scratch,
        compiler_params=PARAMS,
        name="document_heads",
    )(place, in_hbm(query), *own, *anchors, *near, *map(in_hbm, given))


def joined(*scalars):
    return jnp.stack([jnp.asarray(scalar, jnp.int32) for scalar in scalars])


def swapped(values, axis, size, step):
    return lax.ppermute(values, axis, [(place, place ^ step) for place in range(size)])


def question_by_reduction(query, keys, values, prompt_keys, prompt_values, weight):
    row_count = query.shape[0]
    kv_total = keys.shape[1] // HEAD_SIZE
    queries = query.reshape(row_count, kv_total, GROUP_WIDTH, HEAD_SIZE)

    def part(key_block, value_block, visible):
        key_block = key_block.reshape(-1, kv_total, HEAD_SIZE)
        value_block = value_block.reshape(-1, kv_total, HEAD_SIZE)
        scores = FACTOR * jnp.einsum(
            "qhgd,khd->hgqk", queries, key_block, preferred_element_type=jnp.float32
        )
        if visible is not None:
            scores = jnp.where(visible, scores, NEG_INF)
        top = scores.max(axis=3, keepdims=True)
        weights = jnp.exp(scores - top)
        sums = jnp.einsum(
            "hgqk,khd->hgqd",
            weights.astype(jnp.bfloat16),
            value_block,
            preferred_element_type=jnp.float32,
        )
        return top, weights.sum(axis=3, keepdims=True), sums

    ids = jnp.arange(row_count, dtype=jnp.int32)
    block_top, block_total, block_sums = part(keys, values, None)
    self_top, self_total, self_sums = part(prompt_keys, prompt_values, ids[:, None] >= ids[None, :])
    row_top = jnp.maximum(lax.pmax(block_top, "ctx"), self_top)
    scale = jnp.exp(block_top - row_top)
    total, sums = lax.psum((block_total * scale, block_sums * scale), "ctx")
    self_scale = jnp.exp(self_top - row_top)
    attention = (sums + self_sums * self_scale) / (total + self_total * self_scale)
    attention = attention.astype(jnp.bfloat16).transpose(2, 0, 1, 3).reshape(row_count, -1)
    return lax.psum_scatter(
        dot_nn(attention, weight).astype(jnp.bfloat16), "head", scatter_dimension=0, tiled=True
    )


def local(
    ctx_size,
    head_size,
    document_query,
    document_keys,
    document_values,
    question_query,
    prompt_keys,
    prompt_values,
    out_weight,
):
    group = document_keys.shape[1] // HEAD_SIZE
    ring = ctx_size // group
    row_count = question_query.shape[0]
    head_total = question_query.shape[1] // HEAD_SIZE
    position = lax.axis_index("ctx")
    member, turn = position % group, position // group
    place = joined(member, turn, lax.axis_index("head"))

    def in_group(values, step):
        return swapped(values, "ctx", ctx_size, step)

    def in_ring(values, step):
        return swapped(values, "ctx", ctx_size, step * group)

    whole_units = head_total % ctx_size == 0 and group > 1
    question = (question_query, prompt_keys, prompt_values) if whole_units else ()
    sent = range(1, group) if whole_units else range(group)
    own_pieces = list(cut_pieces(place, document_keys, document_values, sent))
    if whole_units:
        own_pieces.insert(0, None)
    pieces = [own_pieces[0]] + [in_group(own_pieces[step], step) for step in range(1, group)]

    half = max(1, group // 2)
    near = ()
    if whole_units:
        near = bring_queries(
            place,
            document_query,
            group,
            range(half),
            question,
            own_pieces[1],
            document_keys,
            document_values,
        )
        arrived, near = lax.optimization_barrier((pieces[1:], near))
        near, question, own_pieces[0] = near[:half], near[half:-1], near[-1]
        pieces = [own_pieces[0], *arrived]

    anchor = lax.select_n(member, *pieces) if group > 1 else pieces[0]

    def sent_on(anchor, reach):
        pairs = [
            (turn_at * group + at, (turn_at + reach) * group + at)
            for turn_at in range(0, ring, 2 * reach)
            for at in range(group)
        ]
        arrived = lax.ppermute(anchor, "ctx", pairs)
        return jnp.where(turn % (2 * reach) == reach, arrived, anchor)

    reach = ring // 2
    if not whole_units:
        while reach:
            anchor = sent_on(anchor, reach)
            reach //= 2
        anchors = [anchor] + [in_group(anchor, step) for step in range(1, group)]
        doc_attention = document_heads(
            place, document_query, group, range(group), own_pieces, anchors, (), (), None, None
        )[0]
        return doc_attention, question_by_reduction(
            question_query, document_keys, document_values, prompt_keys, prompt_values, out_weight
        )

    unit_heads = head_total // ctx_size
    parts = question_parts(place, *question, pieces, ring)
    parts = [parts[0]] + [in_ring(parts[step], step) for step in range(1, ring)]
    while reach > 1:
        anchor = sent_on(anchor, reach)
        reach //= 2
    parts, anchor = lax.optimization_barrier((parts, anchor))
    attention = merge_parts(parts, row_count)
    if reach:
        anchor = sent_on(anchor, reach)
    shards = [attention] + [in_ring(attention, step) for step in range(1, ring)]

    chunks = [(0, step, shards[step], 0) for step in range(ring)]
    both = jnp.concatenate([anchor, attention], axis=0)
    passed = jnp.concatenate(shards[1:], axis=0)
    beside = [in_group(both, step) for step in range(1, group)]
    far = [in_group(passed, step) for step in range(1, group)]
    anchors = [anchor] + beside
    for member_step in range(1, group):
        chunks.append((member_step, 0, beside[member_step - 1], anchor.shape[0]))
        for step in range(1, ring):
            chunks.append(
                (member_step, step, far[member_step - 1], (step - 1) * attention.shape[0])
            )

    doc_attention, calls = None, [range(half), range(half, group)][: 2 if group > 1 else 1]
    for steps in calls:
        last = steps[-1] == group - 1
        doc_attention, *brought = document_heads(
            place,
            document_query,
            group,
            steps,
            [own_pieces[step] for step in steps],
            [anchors[step] for step in steps],
            near,
            () if last else calls[1],
            doc_attention,
            out_weight if last else None,
        )
        near = brought
    (near_weight,) = brought
    shares = project(place, chunks, near_weight, row_count, unit_heads, ring, head_size)
    question_out = shares[0]
    for step in range(1, head_size):
        question_out = question_out + swapped(shares[step], "head", head_size, step).astype(
            jnp.float32
        )
    return doc_attention, question_out.astype(jnp.bfloat16)


def solution(mesh):
    placed = (
        P("ctx", "head"),
        P("ctx", "head"),
        P("ctx", "head"),
        P(None, "head"),
        P(None, "head"),
        P(None, "head"),
        P("head", "ctx"),
    )
    return jax.shard_map(
        functools.partial(local, mesh.shape["ctx"], mesh.shape["head"]),
        mesh=mesh,
        in_specs=placed,
        out_specs=(P("ctx", "head"), P("head", "ctx")),
        check_vma=False,
    )
```
